128 devices in a mesh: dp: 16 (over z, y_hi, core), seq: 8 (over y_lo, x).
Axes of the slice: x: 4, y: 4 (y_hi: 2, y_lo: 2; y = y_hi * 2 + y_lo), z: 4, core: 2. Of those that a mesh axis runs over, the one named last changes fastest.
Arguments:
- tokens: bfloat16 [16, 2048, 640], P('dp', 'seq'), may hold values from -6 to 6
- positions: int32 [16, 2048], P('dp', 'seq'), may hold values from 0 to 1790, as said below
- w_query: bfloat16 [640, 1024], P(('dp', 'seq')), may hold values from -0.25 to 0.25
- w_key: bfloat16 [640, 256], P(('dp', 'seq')), may hold values from -0.25 to 0.25
- w_value: bfloat16 [640, 256], P(('dp', 'seq')), may hold values from -0.25 to 0.25
- w_out: bfloat16 [1024, 640], P(('dp', 'seq')), may hold values from -0.1875 to 0.1875
- w_gate: bfloat16 [640, 2048], P(('dp', 'seq')), may hold values from -0.25 to 0.25
- w_up: bfloat16 [640, 2048], P(('dp', 'seq')), may hold values from -0.25 to 0.25
- w_down: bfloat16 [2048, 640], P(('dp', 'seq')), may hold values from -0.125 to 0.125
- norm_input: bfloat16 [640], P(('dp', 'seq')), may hold values from -0.3984375 to 0.3984375
- norm_post_attn: bfloat16 [640], P(('dp', 'seq')), may hold values from -0.3984375 to 0.3984375
- norm_pre_ff: bfloat16 [640], P(('dp', 'seq')), may hold values from -0.3984375 to 0.3984375
- norm_post_ff: bfloat16 [640], P(('dp', 'seq')), may hold values from -0.3984375 to 0.3984375
- norm_query: bfloat16 [256], P(('dp', 'seq')), may hold values from -0.3984375 to 0.3984375
- norm_key: bfloat16 [256], P(('dp', 'seq')), may hold values from -0.3984375 to 0.3984375
- cotangent: bfloat16 [16, 2048, 640], P('dp', 'seq'), may hold values from -6 to 6
Outputs:
- mixed: bfloat16 [16, 2048, 640], P('dp', 'seq')
- grad_tokens: bfloat16 [16, 2048, 640], P('dp', 'seq')
- grad_w_query: float32 [640, 1024], P(('dp', 'seq'))
- grad_w_key: float32 [640, 256], P(('dp', 'seq'))
- grad_w_value: float32 [640, 256], P(('dp', 'seq'))
- grad_w_out: float32 [1024, 640], P(('dp', 'seq'))
- grad_w_gate: float32 [640, 2048], P(('dp', 'seq'))
- grad_w_up: float32 [640, 2048], P(('dp', 'seq'))
- grad_w_down: float32 [2048, 640], P(('dp', 'seq'))
- grad_norm_input: float32 [640], P(('dp', 'seq'))
- grad_norm_post_attn: float32 [640], P(('dp', 'seq'))
- grad_norm_pre_ff: float32 [640], P(('dp', 'seq'))
- grad_norm_post_ff: float32 [640], P(('dp', 'seq'))
- grad_norm_query: float32 [256], P(('dp', 'seq'))
- grad_norm_key: float32 [256], P(('dp', 'seq'))
The draws below stay inside these ranges and needn't reach their ends.
Inputs may be any that keep to these rules, and one draw needn't show every extreme that they name: Each sequence holds three documents laid end to end; positions count up by one from 0 within each; the first and the last document hold 1 to 256 tokens each and 257 tokens together, so the middle one holds 1791.
All inputs are finite; a program needn't handle non-finite values.
Results may differ from the reference program's by a relative error of at most 0.025.
Values may be sent and summed in bfloat16 or wider, within the bound.
No kernel may reach another device: no remote copies, remote signals or barrier semaphores. Data moves between devices by JAX's collectives and lax.ppermute only.
A program may use at most 192 MiB of HBM per device.

```python
import jax
import jax.numpy as jnp
from jax import lax

D = 640
HEADS = 4
HEAD = 256
FF = 2048
WINDOW = 512
GROUP = 256
LENGTH = 2048
SEQUENCES = 16


def draw_positions(key, part):
    key = jax.random.fold_in(key, 11)
    first_length = jax.random.randint(key, (SEQUENCES, 1), 1, GROUP + 1)
    last_length = GROUP + 1 - first_length
    token_index = jnp.arange(LENGTH, dtype=jnp.int32)[None, :]
    tail_begin = LENGTH - last_length
    begins = jnp.where(token_index < first_length, 0, jnp.where(token_index < tail_begin, first_length, tail_begin))
    return (token_index - begins).astype(jnp.int32)


def level_of(key, shape, shards, smallest, top_value):
    loudness = 1.0
    for axis_at, blocks in shards:
        draws = jax.random.uniform(jax.random.fold_in(jax.random.fold_in(key, 6), axis_at), (blocks,), jnp.float32, smallest / len(shards), top_value / len(shards))
        loudness = loudness * jnp.repeat(jnp.exp(draws), shape[axis_at] // blocks).reshape((-1,) + (1,) * (len(shape) - 1 - axis_at))
    return loudness


def noise(stream_key, shape, spread, most, shards=(), kind=jnp.bfloat16):
    result = spread * jax.random.normal(stream_key, shape, jnp.float32)
    if shards:
        result = result * level_of(stream_key, shape, shards, -0.22, 0.18)
    return jnp.clip(result, -most, most).astype(kind)


def setup_inputs(seed: int = 0) -> dict:
    arg_keys = jax.random.split(jax.random.key(seed), 17)
    return {
        "tokens": noise(arg_keys[0], (SEQUENCES, LENGTH, D), 1.0, 6.0, ((0, 16), (1, 8))),
        "positions": draw_positions(jax.random.fold_in(arg_keys[16], 71), 0),
        "w_query": noise(arg_keys[2], (D, HEADS * HEAD), D ** -0.5, 0.25, ((0, 128),)),
        "w_key": noise(arg_keys[3], (D, HEAD), D ** -0.5, 0.25, ((0, 128),)),
        "w_value": noise(arg_keys[4], (D, HEAD), D ** -0.5, 0.25, ((0, 128),)),
        "w_out": noise(arg_keys[5], (HEADS * HEAD, D), (HEADS * HEAD) ** -0.5, 0.1875, ((0, 128),)),
        "w_gate": noise(arg_keys[6], (D, FF), D ** -0.5, 0.25, ((0, 128),)),
        "w_up": noise(arg_keys[7], (D, FF), D ** -0.5, 0.25, ((0, 128),)),
        "w_down": noise(arg_keys[8], (FF, D), FF ** -0.5, 0.125, ((0, 128),)),
        "norm_input": jnp.clip(jax.random.uniform(arg_keys[9], (D,), jnp.float32, -0.3984375, 0.3984375) * level_of(arg_keys[9], (D,), ((0, 128),), -0.4, 0.0), -0.3984375, 0.3984375).astype(jnp.bfloat16),
        "norm_post_attn": jnp.clip(jax.random.uniform(arg_keys[10], (D,), jnp.float32, -0.3984375, 0.3984375) * level_of(arg_keys[10], (D,), ((0, 128),), -0.4, 0.0), -0.3984375, 0.3984375).astype(jnp.bfloat16),
        "norm_pre_ff": jnp.clip(jax.random.uniform(arg_keys[11], (D,), jnp.float32, -0.3984375, 0.3984375) * level_of(arg_keys[11], (D,), ((0, 128),), -0.4, 0.0), -0.3984375, 0.3984375).astype(jnp.bfloat16),
        "norm_post_ff": jnp.clip(jax.random.uniform(arg_keys[12], (D,), jnp.float32, -0.3984375, 0.3984375) * level_of(arg_keys[12], (D,), ((0, 128),), -0.4, 0.0), -0.3984375, 0.3984375).astype(jnp.bfloat16),
        "norm_query": jnp.clip(jax.random.uniform(arg_keys[13], (HEAD,), jnp.float32, -0.3984375, 0.3984375) * level_of(arg_keys[13], (HEAD,), ((0, 128),), -0.4, 0.0), -0.3984375, 0.3984375).astype(jnp.bfloat16),
        "norm_key": jnp.clip(jax.random.uniform(arg_keys[14], (HEAD,), jnp.float32, -0.3984375, 0.3984375) * level_of(arg_keys[14], (HEAD,), ((0, 128),), -0.4, 0.0), -0.3984375, 0.3984375).astype(jnp.bfloat16),
        "cotangent": noise(arg_keys[15], (SEQUENCES, LENGTH, D), 1.0, 6.0, ((0, 16), (1, 8))),
    }


EPS = 1e-06
HIGH = lax.Precision.HIGHEST
BELOW = -1e+30

@jax.custom_vjp
def low(v):
    return lax.optimization_barrier(v.astype(jnp.bfloat16)).astype(jnp.float32)

@jax.custom_vjp
def low_back(v):
    return v

def low_keep(v):
    return (low(v), None)

def low_pass(kept, grad):
    return (grad,)

def back_keep(v):
    return (v, None)

def back_low(kept, grad):
    return (low(grad),)
low.defvjp(low_keep, low_pass)
low_back.defvjp(back_keep, back_low)

def rms_norm(values, gain):
    return values * lax.rsqrt(lax.optimization_barrier(jnp.mean(values * values, axis=-1, keepdims=True)) + EPS) * (1.0 + gain)

def rotate(values, cosine_table, sine_table):
    half_size = values.shape[-1] // 2
    first_half = values[..., :half_size]
    second = values[..., half_size:]
    return jnp.concatenate([first_half * cosine_table - second * sine_table, second * cosine_table + first_half * sine_table], axis=-1)

def rotary_tables(positions, head_size):
    freq_steps = jnp.arange(head_size // 2).astype(jnp.float32)
    inverse = 10000.0 ** (-2.0 * freq_steps / head_size)
    angles = positions.astype(jnp.float32)[..., None] * inverse
    return (jnp.cos(angles), jnp.sin(angles))

def matmul(left, right):
    return jnp.dot(left, right, precision=HIGH)

def forward_layer(tokens, positions, w_query, w_key, w_value, w_out, w_gate, w_up, w_down, norm_input, norm_post_attn, norm_pre_ff, norm_post_ff, norm_query, norm_key):
    length = tokens.shape[0]
    head_size = norm_key.shape[0]
    head_count = w_query.shape[1] // head_size
    score_scale = head_size ** (-0.5)
    place = positions.astype(jnp.int32)
    cosine_table, sine_table = rotary_tables(place, head_size)
    normed = low(rms_norm(tokens, norm_input))
    query_raw = low_back(matmul(normed, w_query)).reshape(length, head_count, head_size)
    key_raw = low_back(matmul(normed, w_key))
    values = low(low_back(matmul(normed, w_value)))
    queries = low(rotate(rms_norm(query_raw, norm_query), cosine_table[:, None, :], sine_table[:, None, :]))
    key_rows = low(rotate(rms_norm(key_raw, norm_key), cosine_table, sine_table))
    key_pad = jnp.concatenate([jnp.zeros((WINDOW, head_size), key_rows.dtype), key_rows], axis=0)
    value_pad = jnp.concatenate([jnp.zeros((WINDOW, head_size), values.dtype), values], axis=0)
    place_pad = jnp.concatenate([jnp.zeros((WINDOW,), jnp.int32), place], axis=0)

    def attend(block_index):
        begin_at = (block_index * GROUP).astype(jnp.int32)
        block_query = lax.dynamic_slice_in_dim(queries, begin_at, GROUP, 0)
        block_key = lax.dynamic_slice_in_dim(key_pad, begin_at, GROUP + WINDOW, 0)
        block_value = lax.dynamic_slice_in_dim(value_pad, begin_at, GROUP + WINDOW, 0)
        key_place = lax.dynamic_slice_in_dim(place_pad, begin_at, GROUP + WINDOW, 0)
        query_place = lax.dynamic_slice_in_dim(place, begin_at, GROUP, 0)
        query_at = begin_at + jnp.arange(GROUP, dtype=jnp.int32)
        key_at = begin_at - WINDOW + jnp.arange(GROUP + WINDOW, dtype=jnp.int32)
        distance = query_at[:, None] - key_at[None, :]
        allowed = (key_at[None, :] >= 0) & (distance >= 0) & (distance < WINDOW) & (query_place[:, None] - key_place[None, :] == distance)
        raw_scores = low_back(jnp.einsum('qhd,kd->hqk', block_query, block_key, precision=HIGH))
        scores = jnp.where(allowed[None], raw_scores * score_scale, BELOW)
        row_top = lax.optimization_barrier(jnp.max(scores, axis=-1, keepdims=True))
        exps = jnp.exp(scores - row_top)
        probabilities = low(exps / lax.optimization_barrier(jnp.sum(exps, axis=-1, keepdims=True)))
        return jnp.einsum('hqk,kd->qhd', probabilities, block_value, precision=HIGH)
    attended_blocks = lax.map(jax.checkpoint(attend), jnp.arange(length // GROUP, dtype=jnp.int32))
    attended = low_back(low(attended_blocks.reshape(length, head_count * head_size)))
    branch = low_back(matmul(attended, w_out))
    hidden = tokens + rms_norm(branch, norm_post_attn)
    ff_in = low(rms_norm(hidden, norm_pre_ff))
    gate_proj = low_back(matmul(ff_in, w_gate))
    up_proj = low_back(matmul(ff_in, w_up))
    product = low(jax.nn.gelu(gate_proj, approximate=True) * up_proj)
    ff_out = low_back(matmul(product, w_down))
    return hidden + rms_norm(ff_out, norm_post_ff)

def reference(tokens, positions, w_query, w_key, w_value, w_out, w_gate, w_up, w_down, norm_input, norm_post_attn, norm_pre_ff, norm_post_ff, norm_query, norm_key, cotangent):
    params = (w_query, w_key, w_value, w_out, w_gate, w_up, w_down, norm_input, norm_post_attn, norm_pre_ff, norm_post_ff, norm_query, norm_key)
    params = tuple((matrix.astype(jnp.float32) for matrix in params))

    def per_sequence(running, inputs_now):
        seq_tokens, seq_positions, seq_cotangent = inputs_now

        def apply_layer(token_values, *layer_params):
            return forward_layer(token_values, seq_positions, *layer_params)
        output, pullback = jax.vjp(apply_layer, seq_tokens.astype(jnp.float32), *params)
        gradients = pullback(seq_cotangent.astype(jnp.float32))
        running = tuple((running_sum + piece_grad for running_sum, piece_grad in zip(running, gradients[1:])))
        return (running, (output.astype(jnp.bfloat16), gradients[0].astype(jnp.bfloat16)))
    start_sums = tuple((jnp.zeros(matrix.shape, jnp.float32) for matrix in params))
    totals, (outputs, token_grads) = lax.scan(per_sequence, start_sums, (tokens, positions, cotangent))
    return (outputs, token_grads) + tuple(totals)
```

```python
import functools

import jax
import jax.numpy as jnp
import numpy as np
from jax import lax
from jax.experimental import pallas as pl
from jax.experimental.pallas import tpu as pltpu
from jax.sharding import Mesh, PartitionSpec as P

EPS = 1e-06
BELOW = -1e30
WINDOW = 512
ROOT = 0.7978845608028654
CUBE = 0.044715
SIZES = (("z", 4), ("yh", 2), ("core", 2), ("yl", 2), ("x", 4))
AXES = tuple(name for name, _ in SIZES)
DP, SEQ = (AXES[:3], AXES[3:])
NEAR_Z = ("yh", "core", "yl", "x")
NEAR_X = ("z", "yh", "core", "yl")
SWAP = ((0, 1), (1, 0))
GAINS = (5, 5, 5, 5, 2, 2)
BF, F32 = (jnp.bfloat16, jnp.float32)

ROWS = 160
GATE_AT, UP_AT = (768, 2048)


def dot(a, b):
    return jnp.dot(a, b, preferred_element_type=F32)


def dot_tn(a, b):
    return lax.dot_general(a, b, (((0,), (0,)), ((), ())), preferred_element_type=F32)


def dot_nt(a, b):
    return lax.dot_general(a, b, (((1,), (1,)), ((), ())), preferred_element_type=F32)


def panels(ref, base, count, rows):
    return jnp.concatenate(
        [
            jnp.concatenate([ref[z, pl.ds(base + p * rows, rows), :] for z in range(4)], axis=0)
            for p in range(count)
        ],
        axis=1,
    )


def columns(ref, begin, count):
    return jnp.concatenate([ref[p * 640 : (p + 1) * 640, :] for p in range(begin, begin + count)], axis=1)


def put_panels(ref, base, value, rows):
    for p in range(value.shape[1] // 128):
        for z in range(4):
            ref[z, base + p * rows : base + (p + 1) * rows, :] = value[
                z * rows : (z + 1) * rows, p * 128 : (p + 1) * 128
            ].astype(ref.dtype)


def rms(v, gain):
    return v * lax.rsqrt(jnp.mean(v * v, axis=-1, keepdims=True) + EPS) * (1.0 + gain)


def rms_back(v, gain, dy):
    r = lax.rsqrt(jnp.mean(v * v, axis=-1, keepdims=True) + EPS)
    n = v * r
    dn = dy * (1.0 + gain)
    dv = r * (dn - n * jnp.mean(dn * n, axis=-1, keepdims=True))
    return dv, jnp.sum(dy * n, axis=0, keepdims=True)


def turn(v, c, s):
    a, b = (v[:, :128], v[:, 128:])
    return jnp.concatenate([a * c - b * s, b * c + a * s], axis=1)


def turn_back(d, c, s):
    a, b = (d[:, :128], d[:, 128:])
    return jnp.concatenate([a * c + b * s, b * c - a * s], axis=1)


def owner_mask(width, per):
    d = lax.broadcasted_iota(jnp.int32, (128, width), 0) * per
    j = lax.broadcasted_iota(jnp.int32, (128, width), 1)
    return (j >= d) & (j < d + per)


def project_kernel(core_ref, x_ref, own, oth, cos_ref, sin_ref, m5, m2, normed_ref, qraw_ref, kraw_ref, q_ref, kv_ref, gain_ref):
    first = core_ref[0] == 0
    table = own[3840:3968, :]
    wide = dot_tn(table, owner_mask(640, 5).astype(BF))
    thin = dot_tn(table, owner_mask(256, 2).astype(BF))
    lane5 = lax.broadcasted_iota(jnp.int32, (128, 640), 0)
    lane2 = lax.broadcasted_iota(jnp.int32, (128, 256), 0)
    gains = [
        jnp.sum(jnp.where(lane5 == m5[...] + 5 * n, wide, 0.0), axis=0, keepdims=True) for n in range(4)
    ]
    heads = [
        jnp.sum(jnp.where(lane2 == m2[...] + 20 + 2 * n, thin, 0.0), axis=0, keepdims=True) for n in range(2)
    ]
    pad = jnp.zeros((1, 384), F32)
    for n in range(4):
        gain_ref[n : n + 1, :] = gains[n]
    for n in range(2):
        gain_ref[4 + n : 5 + n, :] = jnp.concatenate([heads[n], pad], axis=1)
    gain_ref[6:8, :] = jnp.zeros((2, 640), F32)
    normed = rms(x_ref[...].astype(F32), gains[0]).astype(BF)
    normed_ref[...] = normed
    c, s = (cos_ref[...], sin_ref[...])
    for side, ref in enumerate((own, oth)):
        raw = dot(normed, columns(ref, 0, 4))
        for h in range(2):
            one = raw[:, h * 256 : (h + 1) * 256]
            qraw_ref[2 * side + h] = one
            q_ref[2 * side + h] = turn(rms(one, heads[0]), c, s).astype(BF)
    kv_own, kv_oth = [dot(normed, columns(ref, 4, 2)) for ref in (own, oth)]
    left, right = (jnp.where(first, kv_own, kv_oth), jnp.where(first, kv_oth, kv_own))
    kraw = jnp.concatenate([left[:, :128], right[:, :128]], axis=1)
    kraw_ref[...] = kraw
    kv_ref[:, :256] = turn(rms(kraw, heads[1]), c, s).astype(BF)
    kv_ref[:, 256:384] = left[:, 128:].astype(BF)
    kv_ref[:, 384:] = right[:, 128:].astype(BF)


def allowed_pairs(pos_ref):
    i = lax.broadcasted_iota(jnp.int32, (256, 768), 0)
    j = lax.broadcasted_iota(jnp.int32, (256, 768), 1)
    distance = 512 + i - j
    return (distance >= 0) & (distance <= jnp.minimum(pos_ref[...], WINDOW - 1))


def attend_kernel(q_ref, kv0, kv1, kv2, pos_ref, att_ref, log_ref):
    keys = jnp.concatenate([kv2[:, :256], kv1[:, :256], kv0[:, :256]], axis=0)
    values = jnp.concatenate([kv2[:, 256:], kv1[:, 256:], kv0[:, 256:]], axis=0)
    allowed = allowed_pairs(pos_ref)
    for h in range(4):
        scores = jnp.where(allowed, dot_nt(q_ref[h], keys) * 0.0625, BELOW)
        top = jnp.max(scores, axis=-1, keepdims=True)
        exps = jnp.exp(scores - top)
        total = jnp.sum(exps, axis=-1, keepdims=True)
        att_ref[h] = dot((exps / total).astype(BF), values).astype(BF)
        log_ref[h] = jnp.broadcast_to(top + jnp.log(total), (256, 128))


def gelu_parts(x):
    t = jnp.tanh(ROOT * (x + CUBE * x * x * x))
    half = 0.5 * (1.0 + t)
    return x * half, half + 0.5 * x * (1.0 - t * t) * ROOT * (1.0 + 3.0 * CUBE * x * x)


def feed_kernel(
    core_ref, along_ref, x_ref, g_ref, att_ref, gain_ref, own, oth, d0, d1, d2, d3, e0, e1, e2, e3,
    mixed_ref, dhid_ref, datt_ref, dgain_ref, gff_own, gff_oth, gx_own, gx_oth, wd,
):
    core = core_ref[0]
    along = along_ref[0]
    first = core == 0
    gain_pa, gain_pf, gain_po = [gain_ref[n : n + 1, :] for n in (1, 2, 3)]

    def join(a, b):
        return jnp.where(
            first, jnp.concatenate([a, b[:, 128:]], axis=1), jnp.concatenate([b[:, :256], a], axis=1)
        )

    def part(v):
        low, high = (v[:, :384], v[:, 256:])
        own, oth = (jnp.where(first, low, high), jnp.where(first, high, low))
        lanes = lax.broadcasted_iota(jnp.int32, oth.shape, 1)
        begin = jnp.where(first, 0, 256)
        once = jnp.where((lanes >= begin) & (lanes < begin + 128), 0.0, oth)
        return own.astype(BF), oth.astype(BF), once.astype(BF)

    def out_panels(ref, slot):
        block = lax.rem(slot + 2 * core, 4)
        return jnp.concatenate([ref[block, p * 256 : (p + 1) * 256, :] for p in range(3)], axis=1)

    out_own = [out_panels(own, s) for s in range(4)]
    out_oth = [out_panels(oth, s) for s in range(4)]
    a = sum(dot(att_ref[s], out_own[s]) for s in range(4))
    b = sum(dot(att_ref[s], out_oth[s]) for s in range(4))
    branch = join(a, b)
    hidden = x_ref[...].astype(F32) + rms(branch, gain_pa)
    ff = rms(hidden, gain_pf).astype(BF)

    for side, refs in enumerate(((d0, d1, d2, d3), (e0, e1, e2, e3))):
        for step, ref in enumerate(refs):
            for p in range(3):
                wd[side * 3 + p, :, lax.rem(along + step, 4)] = ref[:, p]

    def down_rows(side, hand):
        begin = lax.rem(core + hand, 2) * 16
        return jnp.concatenate(
            [wd[side * 3 + p, pl.ds(begin, 16)].reshape(1024, 128) for p in range(3)], axis=1
        )

    gates = [panels(ref, GATE_AT, 8, ROWS) for ref in (own, oth)]
    ups = [panels(ref, UP_AT, 8, ROWS) for ref in (own, oth)]
    kept = []
    a = b = 0.0
    for hand in range(2):
        gate, up = (dot(ff, gates[hand]), dot(ff, ups[hand]))
        gelu, slope = gelu_parts(gate)
        product = (gelu * up).astype(BF)
        kept.append((up * slope, gelu, product))
        a = a + dot(product, down_rows(0, hand))
        b = b + dot(product, down_rows(1, hand))
    ff_out = join(a, b)
    mixed_ref[...] = (hidden + rms(ff_out, gain_po)).astype(BF)

    g = g_ref[...].astype(F32)
    d_ff_out, d_po = rms_back(ff_out, gain_po, g)
    d_own, d_oth, d_oth_once = part(d_ff_out)
    d_in = 0.0
    for hand in range(2):
        slope, gelu, product = kept[hand]
        begin = lax.rem(core + hand, 2) * 16
        for ref, d in ((gx_own, d_own), (gx_oth, d_oth)):
            grad = dot_tn(product, d).astype(BF)
            for p in range(3):
                cut = grad[:, p * 128 : (p + 1) * 128].reshape(16, 4, 16, 128)
                for xx in range(4):
                    ref[lax.rem(xx + 4 - along, 4), pl.ds(begin, 16), p] = cut[:, xx]
        d_product = dot_nt(d_own, down_rows(0, hand)) + dot_nt(d_oth_once, down_rows(1, hand))
        d_gate, d_up = ((d_product * slope).astype(BF), (d_product * gelu).astype(BF))
        ref = (gff_own, gff_oth)[hand]
        put_panels(ref, 0, dot_tn(ff, d_gate), ROWS)
        put_panels(ref, UP_AT - GATE_AT, dot_tn(ff, d_up), ROWS)
        d_in = d_in + dot_nt(d_gate, gates[hand]) + dot_nt(d_up, ups[hand])
    d_hidden, d_pf = rms_back(hidden, gain_pf, d_in)
    d_hidden = d_hidden + g
    dhid_ref[...] = d_hidden
    d_branch, d_pa = rms_back(branch, gain_pa, d_hidden)
    d_own, d_oth, d_oth_once = part(d_branch)
    for s in range(4):
        block = lax.rem(s + 2 * core, 4)
        for ref, d in ((gx_own, d_own), (gx_oth, d_oth)):
            grad = dot_tn(att_ref[s], d)
            cut = [grad[:, p * 128 : (p + 1) * 128].reshape(8, 4, 8, 128) for p in range(3)]
            cut.append(jnp.zeros_like(cut[0]))
            for xx in range(4):
                for pair in range(2):
                    rows = jnp.concatenate([cut[2 * pair][:, xx], cut[2 * pair + 1][:, xx]], axis=1)
                    ref[lax.rem(xx + 4 - along, 4), pl.ds(block * 8, 8), 3 + pair] = rows.astype(BF)
        datt_ref[s] = (dot_nt(d_own, out_own[s]) + dot_nt(d_oth_once, out_oth[s])).astype(BF)
    dgain_ref[0:1, :] = d_pa
    dgain_ref[1:2, :] = d_pf
    dgain_ref[2:3, :] = d_po
    dgain_ref[3:8, :] = jnp.zeros((5, 640), F32)


def attend_back_kernel(q_ref, kv0, kv1, kv2, pos_ref, log_ref, datt_ref, dq_ref, dkv0, dkv1, dkv2):
    keys = jnp.concatenate([kv2[:, :256], kv1[:, :256], kv0[:, :256]], axis=0)
    values = jnp.concatenate([kv2[:, 256:], kv1[:, 256:], kv0[:, 256:]], axis=0)
    allowed = allowed_pairs(pos_ref)
    dk = dv = 0.0
    for h in range(4):
        q, d_att = (q_ref[h], datt_ref[h])
        scores = jnp.where(allowed, dot_nt(q, keys) * 0.0625, BELOW)
        probs = jnp.exp(scores - log_ref[h][:, :1])
        dv = dv + dot_tn(probs.astype(BF), d_att)
        d_probs = dot_nt(d_att, values)
        inner = jnp.sum(probs * d_probs, axis=-1, keepdims=True)
        d_scores = (probs * (d_probs - inner) * 0.0625).astype(BF)
        dq_ref[h] = dot(d_scores, keys)
        dk = dk + dot_tn(d_scores, q)
    for n, ref in enumerate((dkv2, dkv1, dkv0)):
        ref[:, :256] = dk[n * 256 : (n + 1) * 256].astype(ref.dtype)
        ref[:, 256:] = dv[n * 256 : (n + 1) * 256].astype(ref.dtype)


def project_back_kernel(
    core_ref, x_ref, normed_ref, qraw_ref, kraw_ref, own, oth, cos_ref, sin_ref, gain_ref, dgain_ref, c5, c2,
    dq_ref, dkv0, dkv1, dkv2, dhid_ref, dx_ref, g_own, g_oth,
):
    first = core_ref[0] == 0
    c, s = (cos_ref[...], sin_ref[...])
    normed = normed_ref[...]
    gain_q, gain_k = (gain_ref[4:5, :256], gain_ref[5:6, :256])
    dkv = dkv0[...] + dkv1[...].astype(F32) + dkv2[...].astype(F32)
    d_k, d_gain_k = rms_back(kraw_ref[...], gain_k, turn_back(dkv[:, :256], c, s))
    d_k, d_v = (d_k.astype(BF), dkv[:, 256:].astype(BF))
    left = jnp.concatenate([d_k[:, :128], d_v[:, :128]], axis=1)
    right = jnp.concatenate([d_k[:, 128:], d_v[:, 128:]], axis=1)
    sides = (jnp.where(first, left, right), jnp.where(first, right, left))
    feature = lax.broadcasted_iota(jnp.int32, (640, 128), 0)
    owner = lax.broadcasted_iota(jnp.int32, (640, 128), 1)
    by_row = [dot(normed, (feature == 5 * owner + r).astype(F32).astype(BF)).astype(BF) for r in range(5)]
    d_gain_q = 0.0
    d_normed = 0.0
    for side, (w, ref) in enumerate(((own, g_own), (oth, g_oth))):
        d_qs = []
        for h in range(2):
            d, dg = rms_back(qraw_ref[2 * side + h], gain_q, turn_back(dq_ref[2 * side + h], c, s))
            d_gain_q = d_gain_q + dg
            d_qs.append(d.astype(BF))
        d_q = jnp.concatenate(d_qs, axis=1)
        d_all = jnp.concatenate([d_q, sides[side]], axis=1)
        for r in range(5):
            grad = dot_tn(by_row[r], d_all)
            for p in range(6):
                ref[pl.ds(5 * p + r, 128, stride=32), :] = grad[:, p * 128 : (p + 1) * 128]
        d_normed = d_normed + dot_nt(d_q, columns(w, 0, 4)) + dot_nt(sides[side], columns(w, 4, 2))
    dx, d_in = rms_back(x_ref[...].astype(F32), gain_ref[0:1, :], d_normed)
    dx_ref[...] = (dx + dhid_ref[...]).astype(BF)
    mask5, mask2 = (owner_mask(640, 5), owner_mask(256, 2))
    lane5 = lax.broadcasted_iota(jnp.int32, (640, 128), 1)
    lane2 = lax.broadcasted_iota(jnp.int32, (256, 128), 1)
    table = 0.0
    for n, d in enumerate((d_in, dgain_ref[0:1, :], dgain_ref[1:2, :], dgain_ref[2:3, :])):
        place = (lane5 == c5[...] + 5 * n).astype(F32).astype(BF)
        table = table + dot(jnp.where(mask5, d, 0.0).astype(BF), place)
    for n, d in enumerate((d_gain_q, d_gain_k)):
        place = (lane2 == c2[...] + 20 + 2 * n).astype(F32).astype(BF)
        table = table + dot(jnp.where(mask2, d, 0.0).astype(BF), place)
    for ref in (g_own, g_oth):
        ref[pl.ds(30, 128, stride=32), :] = table
        ref[pl.ds(31, 128, stride=32), :] = jnp.zeros_like(table)


def call(kernel, outs, args, scratch=(), name=None):
    vmem = pl.BlockSpec(memory_space=pltpu.VMEM)
    smem = pl.BlockSpec(memory_space=pltpu.SMEM)
    return pl.pallas_call(
        kernel,
        out_shape=[jax.ShapeDtypeStruct(shape, dtype) for shape, dtype in outs],
        in_specs=[smem if a.shape == (1,) else vmem for a in args],
        out_specs=[vmem] * len(outs),
        scratch_shapes=list(scratch),
        compiler_params=pltpu.CompilerParams(vmem_limit_bytes=60 * 1024 * 1024),
        name=name,
    )(*args)


def halves(a):
    rows, width = a.shape
    if width % 256:
        cut = a.reshape(rows, -1, 128).transpose(1, 0, 2)
        part = (width + 128) // 256
        return jnp.stack([cut[:part], cut[-part:]]).reshape(2, -1, 128)
    return a.reshape(rows, 2, -1, 128).transpose(1, 2, 0, 3).reshape(2, -1, 128)


def to_all(flat, before, after):
    wide = jnp.broadcast_to(flat[None, :, None], (before, 2, after, *flat.shape[1:]))
    return wide.reshape(-1, *flat.shape[1:])


def block_of(near, at, panel_count, rows):
    cut = near[:, at : at + panel_count * rows].reshape(-1, panel_count, rows, 128)
    return cut.transpose(1, 0, 2, 3).reshape(-1, 128)


def pieces_of(block, panel_count, rows):
    cut = block.reshape(panel_count, -1, rows, 128)
    return cut.transpose(1, 0, 2, 3).reshape(cut.shape[1], -1, 128)


def whole(cut, panel_count, rows, width):
    cut = cut.reshape(2, panel_count, rows, 128)
    if width % 256:
        cut = jnp.concatenate([cut[0, : width // 128 - panel_count], cut[1]], axis=0)
        return cut.transpose(1, 0, 2).reshape(rows, width)
    return cut.transpose(2, 0, 1, 3).reshape(rows, width)


def body(
    tokens, positions, w_query, w_key, w_value, w_out, w_gate, w_up, w_down,
    norm_input, norm_post_attn, norm_pre_ff, norm_post_ff, norm_query, norm_key, cotangent,
):
    core, along_x = [lax.axis_index(a).astype(jnp.int32).reshape(1) for a in ("core", "x")]
    x = tokens.reshape(256, 640)
    g = cotangent.reshape(256, 640)
    place = positions.reshape(256, 1)
    steps = jnp.arange(128).astype(F32)
    angles = place.astype(F32) * (10000.0 ** (-2.0 * steps / 256))
    cos, sin = (jnp.cos(angles), jnp.sin(angles))
    m5, m2 = [jnp.asarray((np.arange(n) % k).astype(np.int32)) for n, k in ((640, 5), (256, 2))]

    gain_row = jnp.concatenate([norm_input, norm_post_attn, norm_pre_ff, norm_post_ff, norm_query, norm_key])
    gain_row = jnp.pad(gain_row, (0, 104)).reshape(1, 1, 128)
    flat = jnp.concatenate(
        [halves(w_query), halves(w_key), halves(w_value), jnp.broadcast_to(gain_row, (2, 1, 128))], axis=1
    )
    flat_ff = jnp.concatenate([halves(w_out), halves(w_gate), halves(w_up)], axis=1)
    near = lax.all_to_all(to_all(flat_ff, 2, 8), NEAR_Z, 0, 0)
    near, flat_down, flat = lax.optimization_barrier((near, halves(w_down), flat))
    block = jnp.concatenate([block_of(near, 0, 3, 8), block_of(near, 24, 8, 5), block_of(near, 64, 8, 5)])
    f_own = lax.all_gather(block, "z")

    near = lax.all_to_all(to_all(flat_down, 8, 2), NEAR_X, 0, 0).reshape(32, 3, 16, 128)
    near, flat = lax.optimization_barrier((near, flat))
    d_own = [near] + [lax.ppermute(near, "x", [((i + d) % 4, i) for i in range(4)]) for d in (1, 3, 2)]
    d_own = [d_own[i] for i in (0, 1, 3, 2)]

    near = lax.all_to_all(to_all(flat, 8, 8), AXES, 0, 0)
    q_own = jnp.concatenate(
        [block_of(near, 0, 4, 5), block_of(near, 20, 1, 5), block_of(near, 25, 1, 5), near[:, 30]]
    )
    q_own, d_own[1], d_own[3] = lax.optimization_barrier((q_own, d_own[1], d_own[3]))
    q_oth = lax.ppermute(q_own, "core", SWAP)

    normed, q_raw, k_raw, q, kv, gains = call(
        project_kernel,
        [((256, 640), BF), ((4, 256, 256), F32), ((256, 256), F32), ((4, 256, 256), BF), ((256, 512), BF), ((8, 640), F32)],
        (core, x, q_own, q_oth, cos, sin, m5.reshape(1, 640), m2.reshape(1, 256)),
        name="project",
    )

    def along(v, distance):
        return lax.ppermute(v, SEQ, [(i - distance, i) for i in range(8) if 0 <= i - distance < 8])

    kv1, kv2 = (along(kv, 1), along(kv, 2))
    kv1, kv2, f_own, *d_own = lax.optimization_barrier((kv1, kv2, f_own, *d_own))
    f_oth = lax.ppermute(f_own, "core", SWAP)
    d_oth = [lax.ppermute(d, "core", SWAP) for d in d_own]
    attended, log_total = call(
        attend_kernel,
        [((4, 256, 256), BF), ((4, 256, 128), F32)],
        (q, kv, kv1, kv2, place),
        name="attend",
    )
    mixed, d_hidden, d_att, d_gains, gff_own, gff_oth, gx_own, gx_oth = call(
        feed_kernel,
        [((256, 640), BF), ((256, 640), F32), ((4, 256, 256), BF), ((8, 640), F32)]
        + [((4, 2560, 128), BF)] * 2 + [((4, 32, 5, 16, 128), BF)] * 2,
        (core, along_x, x, g, attended, gains, f_own, f_oth, *d_own, *d_oth),
        scratch=(pltpu.VMEM((6, 32, 4, 16, 128), BF),),
        name="feed",
    )

    def both(mine, theirs):
        return (mine.astype(F32) + lax.ppermute(theirs.astype(BF), "core", SWAP).astype(F32)).astype(BF)

    gff, gx = (both(gff_own, gff_oth), both(gx_own, gx_oth))

    d_q, dkv0, dkv1, dkv2 = call(
        attend_back_kernel,
        [((4, 256, 256), F32), ((256, 512), F32), ((256, 512), BF), ((256, 512), BF)],
        (q, kv, kv1, kv2, place, log_total, d_att),
        name="attend_back",
    )
    dkv1, dkv2 = (along(dkv1, -1), along(dkv2, -2))
    dkv1, dkv2, gff, gx = lax.optimization_barrier((dkv1, dkv2, gff, gx))
    gff_near = lax.psum_scatter(gff, "z")
    gx_near = gx[0].astype(F32)
    gx_1, gx_3, gx_2 = [lax.ppermute(gx[d], "x", [(i, (i + d) % 4) for i in range(4)]) for d in (1, 3, 2)]
    d_x, gq_own, gq_oth = call(
        project_back_kernel,
        [((256, 640), BF)] + [((4096, 128), F32)] * 2,
        (core, x, normed, q_raw, k_raw, q_own, q_oth, cos, sin, gains, d_gains, m5.reshape(640, 1), m2.reshape(256, 1),
         d_q, dkv0, dkv1, dkv2, d_hidden),
        name="project_back",
    )
    gq_oth, gx_1, gx_2, gx_3 = lax.optimization_barrier((gq_oth.astype(BF), gx_1, gx_2, gx_3))
    gq = both(gq_own, gq_oth)
    gx_near = gx_near + gx_1.astype(F32) + gx_2.astype(F32) + gx_3.astype(F32)
    gx_near = gx_near.astype(BF)

    def total(back, before, after):
        return back.reshape(before, 2, after, *back.shape[1:]).astype(F32).sum((0, 2))

    ff = jnp.concatenate([pieces_of(gff_near[:1280], 8, 5), pieces_of(gff_near[1280:], 8, 5)], axis=1)
    qkv = lax.all_to_all(gq.reshape(128, 32, 128), AXES, 0, 0)
    qkv, gx_near = lax.optimization_barrier((qkv, gx_near))
    gx_all = lax.all_to_all(gx_near.reshape(32, 80, 128), NEAR_X, 0, 0)
    gx_all, ff = lax.optimization_barrier((gx_all, ff))
    ff = lax.all_to_all(ff, NEAR_Z, 0, 0)
    qkv, gx_all, ff = (total(qkv, 8, 8), total(gx_all, 8, 2), total(ff, 2, 8))
    grads = [
        whole(qkv[:, :20], 4, 5, 1024),
        whole(qkv[:, 20:25], 1, 5, 256),
        whole(qkv[:, 25:30], 1, 5, 256),
        whole(gx_all[:, 48:72], 3, 8, 640),
        whole(ff[:, :40], 8, 5, 2048),
        whole(ff[:, 40:], 8, 5, 2048),
        whole(gx_all[:, :48], 3, 16, 640),
    ]
    at = 0
    for n in GAINS:
        grads.append(qkv[0, 30, at : at + n])
        at += n
    return (mixed.reshape(1, 256, 640), d_x.reshape(1, 256, 640), *grads)


def solution(mesh):
    fine = Mesh(mesh.devices.reshape([size for _, size in SIZES]), AXES)
    rows, lines, wide, flat = (P(DP, SEQ, None), P(DP, SEQ), P(AXES, None), P(AXES))
    return jax.shard_map(
        body,
        mesh=fine,
        in_specs=(rows, lines) + (wide,) * 7 + (flat,) * 6 + (rows,),
        out_specs=(rows, rows) + (wide,) * 7 + (flat,) * 6,
        check_vma=False,
    )
```

```python
import functools

import jax
import jax.numpy as jnp
import numpy as np
from jax import lax
from jax.experimental import pallas as pl
from jax.experimental.pallas import tpu as pltpu
from jax.sharding import Mesh, PartitionSpec as P

EPS = 1e-06
BELOW = -1e30
WINDOW = 512
ROOT = 0.7978845608028654
CUBE = 0.044715
SIZES = (("z", 4), ("yh", 2), ("core", 2), ("yl", 2), ("x", 4))
AXES = tuple(name for name, _ in SIZES)
DP, SEQ = (AXES[:3], AXES[3:])
NEAR_Z = ("yh", "core", "yl", "x")
NEAR_Y = ("z", "core", "x")
Y = ("yh", "yl")
SWAP = ((0, 1), (1, 0))
GAINS = (5, 5, 5, 5, 2, 2)
BF, F32 = (jnp.bfloat16, jnp.float32)

ROWS = 160
GATE_AT, UP_AT = (768, 2048)


def dot(a, b):
    return jnp.dot(a, b, preferred_element_type=F32)


def dot_tn(a, b):
    return lax.dot_general(a, b, (((0,), (0,)), ((), ())), preferred_element_type=F32)


def dot_nt(a, b):
    return lax.dot_general(a, b, (((1,), (1,)), ((), ())), preferred_element_type=F32)


def panels(ref, base, count, rows):
    return jnp.concatenate(
        [
            jnp.concatenate([ref[z, pl.ds(base + p * rows, rows), :] for z in range(4)], axis=0)
            for p in range(count)
        ],
        axis=1,
    )


def columns(ref, begin, count):
    return jnp.concatenate([ref[p * 640 : (p + 1) * 640, :] for p in range(begin, begin + count)], axis=1)


def put_panels(ref, base, value, rows):
    for p in range(value.shape[1] // 128):
        for z in range(4):
            ref[z, base + p * rows : base + (p + 1) * rows, :] = value[
                z * rows : (z + 1) * rows, p * 128 : (p + 1) * 128
            ].astype(ref.dtype)


def rms(v, gain):
    return v * lax.rsqrt(jnp.mean(v * v, axis=-1, keepdims=True) + EPS) * (1.0 + gain)


def rms_back(v, gain, dy):
    r = lax.rsqrt(jnp.mean(v * v, axis=-1, keepdims=True) + EPS)
    n = v * r
    dn = dy * (1.0 + gain)
    dv = r * (dn - n * jnp.mean(dn * n, axis=-1, keepdims=True))
    return dv, jnp.sum(dy * n, axis=0, keepdims=True)


def turn(v, c, s):
    a, b = (v[:, :128], v[:, 128:])
    return jnp.concatenate([a * c - b * s, b * c + a * s], axis=1)


def turn_back(d, c, s):
    a, b = (d[:, :128], d[:, 128:])
    return jnp.concatenate([a * c + b * s, b * c - a * s], axis=1)


def owner_mask(width, per):
    d = lax.broadcasted_iota(jnp.int32, (128, width), 0) * per
    j = lax.broadcasted_iota(jnp.int32, (128, width), 1)
    return (j >= d) & (j < d + per)


def allowed_pairs(pos_ref):
    i = lax.broadcasted_iota(jnp.int32, (256, 768), 0)
    j = lax.broadcasted_iota(jnp.int32, (256, 768), 1)
    distance = 512 + i - j
    return (distance >= 0) & (distance <= jnp.minimum(pos_ref[...], WINDOW - 1))


def attend_kernel(
    core_ref, x0, x1, x2, own, oth, cos_ref, sin_ref, pos_ref, m5, m2,
    normed_ref, qraw_ref, kraw_ref, q_ref, kv_ref, gain_ref, att_ref, log_ref,
):
    first = core_ref[0] == 0
    table = own[3840:3968, :]
    wide = dot_tn(table, owner_mask(640, 5).astype(BF))
    thin = dot_tn(table, owner_mask(256, 2).astype(BF))
    lane5 = lax.broadcasted_iota(jnp.int32, (128, 640), 0)
    lane2 = lax.broadcasted_iota(jnp.int32, (128, 256), 0)
    gains = [
        jnp.sum(jnp.where(lane5 == m5[...] + 5 * n, wide, 0.0), axis=0, keepdims=True) for n in range(4)
    ]
    heads = [
        jnp.sum(jnp.where(lane2 == m2[...] + 20 + 2 * n, thin, 0.0), axis=0, keepdims=True) for n in range(2)
    ]
    pad = jnp.zeros((1, 384), F32)
    for n in range(4):
        gain_ref[n : n + 1, :] = gains[n]
    for n in range(2):
        gain_ref[4 + n : 5 + n, :] = jnp.concatenate([heads[n], pad], axis=1)
    gain_ref[6:8, :] = jnp.zeros((2, 640), F32)
    for n, ref in enumerate((x2, x1, x0)):
        normed_ref[n * 256 : (n + 1) * 256, :] = rms(ref[...].astype(F32), gains[0]).astype(BF)
    normed = normed_ref[...]
    c, s = (cos_ref[...], sin_ref[...])
    kv_own, kv_oth = [dot(normed, columns(ref, 4, 2)) for ref in (own, oth)]
    left, right = (jnp.where(first, kv_own, kv_oth), jnp.where(first, kv_oth, kv_own))
    kraw = jnp.concatenate([left[:, :128], right[:, :128]], axis=1)
    kraw_ref[...] = kraw
    keys = turn(rms(kraw, heads[1]), c, s).astype(BF)
    values = jnp.concatenate([left[:, 128:], right[:, 128:]], axis=1).astype(BF)
    kv_ref[:, :256] = keys
    kv_ref[:, 256:] = values
    c, s = (c[512:], s[512:])
    allowed = allowed_pairs(pos_ref)
    for side, ref in enumerate((own, oth)):
        raw = dot(normed_ref[512:, :], columns(ref, 0, 4))
        for h in range(2):
            slot = 2 * side + h
            one = raw[:, h * 256 : (h + 1) * 256]
            qraw_ref[slot] = one
            q = turn(rms(one, heads[0]), c, s).astype(BF)
            q_ref[slot] = q
            scores = jnp.where(allowed, dot_nt(q, keys) * 0.0625, BELOW)
            top = jnp.max(scores, axis=-1, keepdims=True)
            exps = jnp.exp(scores - top)
            total = jnp.sum(exps, axis=-1, keepdims=True)
            att_ref[slot] = dot((exps / total).astype(BF), values).astype(BF)
            log_ref[slot] = jnp.broadcast_to(top + jnp.log(total), (256, 128))


def gelu_parts(x):
    t = jnp.tanh(ROOT * (x + CUBE * x * x * x))
    half = 0.5 * (1.0 + t)
    return x * half, half + 0.5 * x * (1.0 - t * t) * ROOT * (1.0 + 3.0 * CUBE * x * x)


def feed_kernel(
    core_ref, x_ref, g_ref, att_ref, gain_ref, own, oth, down_own, down_oth,
    mixed_ref, dhid_ref, datt_ref, dgain_ref, gff_own, gff_oth, gx_own, gx_oth,
):
    core = core_ref[0]
    first = core == 0
    gain_pa, gain_pf, gain_po = [gain_ref[n : n + 1, :] for n in (1, 2, 3)]

    def join(a, b):
        return jnp.where(
            first, jnp.concatenate([a, b[:, 128:]], axis=1), jnp.concatenate([b[:, :256], a], axis=1)
        )

    def part(v):
        low, high = (v[:, :384], v[:, 256:])
        own, oth = (jnp.where(first, low, high), jnp.where(first, high, low))
        lanes = lax.broadcasted_iota(jnp.int32, oth.shape, 1)
        begin = jnp.where(first, 0, 256)
        once = jnp.where((lanes >= begin) & (lanes < begin + 128), 0.0, oth)
        return own.astype(BF), oth.astype(BF), once.astype(BF)

    def out_panels(ref, slot):
        block = lax.rem(slot + 2 * core, 4)
        return jnp.concatenate([ref[block, p * 256 : (p + 1) * 256, :] for p in range(3)], axis=1)

    out_own = [out_panels(own, s) for s in range(4)]
    out_oth = [out_panels(oth, s) for s in range(4)]
    a = sum(dot(att_ref[s], out_own[s]) for s in range(4))
    b = sum(dot(att_ref[s], out_oth[s]) for s in range(4))
    branch = join(a, b)
    hidden = x_ref[...].astype(F32) + rms(branch, gain_pa)
    ff = rms(hidden, gain_pf).astype(BF)

    def down_rows(ref, hand):
        begin = lax.rem(core + hand, 2) * 64
        return jnp.concatenate(
            [ref[pl.ds(begin, 64), p * 16 : (p + 1) * 16].reshape(1024, 128) for p in range(3)], axis=1
        )

    gates = [panels(ref, GATE_AT, 8, ROWS) for ref in (own, oth)]
    ups = [panels(ref, UP_AT, 8, ROWS) for ref in (own, oth)]
    kept = []
    a = b = 0.0
    for hand in range(2):
        gate, up = (dot(ff, gates[hand]), dot(ff, ups[hand]))
        gelu, slope = gelu_parts(gate)
        product = (gelu * up).astype(BF)
        kept.append((up * slope, gelu, product))
        a = a + dot(product, down_rows(down_own, hand))
        b = b + dot(product, down_rows(down_oth, hand))
    ff_out = join(a, b)
    mixed_ref[...] = (hidden + rms(ff_out, gain_po)).astype(BF)

    g = g_ref[...].astype(F32)
    d_ff_out, d_po = rms_back(ff_out, gain_po, g)
    d_own, d_oth, d_oth_once = part(d_ff_out)
    d_in = 0.0
    for hand in range(2):
        slope, gelu, product = kept[hand]
        begin = lax.rem(core + hand, 2) * 64
        for ref, d in ((gx_own, d_own), (gx_oth, d_oth)):
            grad = dot_tn(product, d).astype(BF)
            for p in range(3):
                cut = grad[:, p * 128 : (p + 1) * 128].reshape(64, 16, 128)
                ref[pl.ds(begin, 64), p * 16 : (p + 1) * 16] = cut
        d_product = dot_nt(d_own, down_rows(down_own, hand)) + dot_nt(d_oth_once, down_rows(down_oth, hand))
        d_gate, d_up = ((d_product * slope).astype(BF), (d_product * gelu).astype(BF))
        ref = (gff_own, gff_oth)[hand]
        put_panels(ref, 0, dot_tn(ff, d_gate), ROWS)
        put_panels(ref, UP_AT - GATE_AT, dot_tn(ff, d_up), ROWS)
        d_in = d_in + dot_nt(d_gate, gates[hand]) + dot_nt(d_up, ups[hand])
    d_hidden, d_pf = rms_back(hidden, gain_pf, d_in)
    d_hidden = d_hidden + g
    dhid_ref[...] = d_hidden
    d_branch, d_pa = rms_back(branch, gain_pa, d_hidden)
    d_own, d_oth, d_oth_once = part(d_branch)
    for s in range(4):
        block = lax.rem(s + 2 * core, 4)
        for ref, d in ((gx_own, d_own), (gx_oth, d_oth)):
            grad = dot_tn(att_ref[s], d)
            cut = [grad[:, p * 128 : (p + 1) * 128].reshape(32, 8, 128) for p in range(3)]
            cut.append(jnp.zeros_like(cut[0]))
            for pair in range(2):
                rows = jnp.concatenate(cut[2 * pair : 2 * pair + 2], axis=1)
                ref[pl.ds(block * 32, 32), 48 + pair * 16 : 64 + pair * 16] = rows.astype(BF)
        datt_ref[s] = (dot_nt(d_own, out_own[s]) + dot_nt(d_oth_once, out_oth[s])).astype(BF)
    dgain_ref[0:1, :] = d_pa
    dgain_ref[1:2, :] = d_pf
    dgain_ref[2:3, :] = d_po
    dgain_ref[3:8, :] = jnp.zeros((5, 640), F32)


def attend_back_kernel(q_ref, kv_ref, pos_ref, log_ref, datt_ref, dq_ref, dkv_ref):
    keys, values = (kv_ref[:, :256], kv_ref[:, 256:])
    allowed = allowed_pairs(pos_ref)
    dk = dv = 0.0
    for h in range(4):
        q, d_att = (q_ref[h], datt_ref[h])
        scores = jnp.where(allowed, dot_nt(q, keys) * 0.0625, BELOW)
        probs = jnp.exp(scores - log_ref[h][:, :1])
        dv = dv + dot_tn(probs.astype(BF), d_att)
        d_probs = dot_nt(d_att, values)
        inner = jnp.sum(probs * d_probs, axis=-1, keepdims=True)
        d_scores = (probs * (d_probs - inner) * 0.0625).astype(BF)
        dk = dk + dot_tn(d_scores, q)
        dq_ref[h] = dot(d_scores, keys)
    dkv_ref[:, :256] = dk
    dkv_ref[:, 256:] = dv


def project_back_kernel(
    core_ref, x0, x1, x2, normed_ref, qraw_ref, kraw_ref, own, oth, cos_ref, sin_ref, gain_ref, dgain_ref, c5, c2,
    dq_ref, dkv_ref, dhid_ref, dx0, dx1, dx2, g_own, g_oth,
):
    first = core_ref[0] == 0
    c, s = (cos_ref[...], sin_ref[...])
    gain_q, gain_k = (gain_ref[4:5, :256], gain_ref[5:6, :256])
    dk, dv = (dkv_ref[:, :256], dkv_ref[:, 256:])
    d_gain_q = 0.0
    d_qs = []
    for h in range(4):
        d, dg = rms_back(qraw_ref[h], gain_q, turn_back(dq_ref[h], c[512:], s[512:]))
        d_gain_q = d_gain_q + dg
        d_qs.append(d.astype(BF))
    d_k, d_gain_k = rms_back(kraw_ref[...], gain_k, turn_back(dk, c, s))
    left = jnp.concatenate([d_k[:, :128], dv[:, :128]], axis=1)
    right = jnp.concatenate([d_k[:, 128:], dv[:, 128:]], axis=1)
    sides = (jnp.where(first, left, right).astype(BF), jnp.where(first, right, left).astype(BF))
    d_query = d_normed = 0.0
    for side, (w, ref) in enumerate(((own, g_own), (oth, g_oth))):
        d_q = jnp.concatenate(d_qs[2 * side : 2 * side + 2], axis=1)
        put_panels(ref, 0, dot_tn(normed_ref[512:, :], d_q), ROWS)
        put_panels(ref, 4 * ROWS, dot_tn(normed_ref[...], sides[side]), ROWS)
        d_query = d_query + dot_nt(d_q, columns(w, 0, 4))
        d_normed = d_normed + dot_nt(sides[side], columns(w, 4, 2))
    d_in = 0.0
    for n, (x_ref, out) in enumerate(((x2, dx2), (x1, dx1), (x0, dx0))):
        d = d_normed[n * 256 : (n + 1) * 256]
        if n == 2:
            d = d + d_query
        dx, dg = rms_back(x_ref[...].astype(F32), gain_ref[0:1, :], d)
        d_in = d_in + dg
        out[...] = (dx + dhid_ref[...] if n == 2 else dx).astype(out.dtype)
    mask5, mask2 = (owner_mask(640, 5), owner_mask(256, 2))
    lane5 = lax.broadcasted_iota(jnp.int32, (640, 128), 1)
    lane2 = lax.broadcasted_iota(jnp.int32, (256, 128), 1)
    table = 0.0
    for n, d in enumerate((d_in, dgain_ref[0:1, :], dgain_ref[1:2, :], dgain_ref[2:3, :])):
        place = (lane5 == c5[...] + 5 * n).astype(F32).astype(BF)
        table = table + dot(jnp.where(mask5, d, 0.0).astype(BF), place)
    for n, d in enumerate((d_gain_q, d_gain_k)):
        place = (lane2 == c2[...] + 20 + 2 * n).astype(F32).astype(BF)
        table = table + dot(jnp.where(mask2, d, 0.0).astype(BF), place)
    feature = lax.broadcasted_iota(jnp.int32, (640, 128), 0)
    owner = lax.broadcasted_iota(jnp.int32, (640, 128), 1)
    table = dot((feature == 5 * owner).astype(F32).astype(BF), table.astype(BF))
    for ref in (g_own, g_oth):
        put_panels(ref, 6 * ROWS, table, ROWS)


def call(kernel, outs, args, scratch=(), name=None):
    vmem = pl.BlockSpec(memory_space=pltpu.VMEM)
    smem = pl.BlockSpec(memory_space=pltpu.SMEM)
    return pl.pallas_call(
        kernel,
        out_shape=[jax.ShapeDtypeStruct(shape, dtype) for shape, dtype in outs],
        in_specs=[smem if a.shape == (1,) else vmem for a in args],
        out_specs=[vmem] * len(outs),
        scratch_shapes=list(scratch),
        compiler_params=pltpu.CompilerParams(vmem_limit_bytes=60 * 1024 * 1024),
        name=name,
    )(*args)


def halves(a):
    rows, width = a.shape
    if width % 256:
        cut = a.reshape(rows, -1, 128).transpose(1, 0, 2)
        part = (width + 128) // 256
        return jnp.stack([cut[:part], cut[-part:]]).reshape(2, -1, 128)
    return a.reshape(rows, 2, -1, 128).transpose(1, 2, 0, 3).reshape(2, -1, 128)


def to_all(flat, before, after):
    wide = jnp.broadcast_to(flat[None, :, None], (before, 2, after, *flat.shape[1:]))
    return wide.reshape(-1, *flat.shape[1:])


def block_of(near, at, panel_count, rows):
    cut = near[:, at : at + panel_count * rows].reshape(-1, panel_count, rows, 128)
    return cut.transpose(1, 0, 2, 3).reshape(-1, 128)


def pieces_of(block, panel_count, rows):
    cut = block.reshape(panel_count, -1, rows, 128)
    return cut.transpose(1, 0, 2, 3).reshape(cut.shape[1], -1, 128)


def whole(cut, panel_count, rows, width):
    cut = cut.reshape(2, panel_count, rows, 128)
    if width % 256:
        cut = jnp.concatenate([cut[0, : width // 128 - panel_count], cut[1]], axis=0)
        return cut.transpose(1, 0, 2).reshape(rows, width)
    return cut.transpose(2, 0, 1, 3).reshape(rows, width)


def body(
    tokens, positions, w_query, w_key, w_value, w_out, w_gate, w_up, w_down,
    norm_input, norm_post_attn, norm_pre_ff, norm_post_ff, norm_query, norm_key, cotangent,
):
    core = lax.axis_index("core").astype(jnp.int32).reshape(1)
    x = tokens.reshape(256, 640)
    g = cotangent.reshape(256, 640)

    def along(v, distance):
        return lax.ppermute(v, SEQ, [(i - distance, i) for i in range(8) if 0 <= i - distance < 8])

    x1, x2 = (along(x, 1), along(x, 2))
    place = positions.reshape(256, 1)
    before = positions[:, :1] - jnp.arange(512, 0, -1, dtype=jnp.int32)[None]
    places = jnp.concatenate([before, positions], axis=1).reshape(768, 1)
    steps = jnp.arange(128).astype(F32)
    angles = places.astype(F32) * (10000.0 ** (-2.0 * steps / 256))
    cos, sin = (jnp.cos(angles), jnp.sin(angles))
    m5, m2 = [jnp.asarray((np.arange(n) % k).astype(np.int32)) for n, k in ((640, 5), (256, 2))]

    gain_row = jnp.concatenate([norm_input, norm_post_attn, norm_pre_ff, norm_post_ff, norm_query, norm_key])
    gain_row = jnp.pad(gain_row, (0, 104)).reshape(1, 1, 128)
    flat = jnp.concatenate(
        [halves(w_query), halves(w_key), halves(w_value), jnp.broadcast_to(gain_row, (2, 1, 128))], axis=1
    )
    flat_ff = jnp.concatenate([halves(w_out), halves(w_gate), halves(w_up)], axis=1)
    near = lax.all_to_all(to_all(flat_ff, 2, 8), NEAR_Z, 0, 0)
    flat = jnp.concatenate([halves(w_down), flat], axis=1)
    near, flat, cos, sin, place = lax.optimization_barrier((near, flat, cos, sin, place))
    block = jnp.concatenate([block_of(near, 0, 3, 8), block_of(near, 24, 8, 5), block_of(near, 64, 8, 5)])
    f_own = lax.all_gather(block, "z")

    near = lax.all_to_all(to_all(flat, 8, 8), AXES, 0, 0)
    q_own = jnp.concatenate(
        [block_of(near, 48, 4, 5), block_of(near, 68, 1, 5), block_of(near, 73, 1, 5), near[:, 78]]
    )
    q_own, x1, x2 = lax.optimization_barrier((q_own, x1, x2))
    q_oth = lax.ppermute(q_own, "core", SWAP)
    d_own = near[:, :48]
    d_oth = lax.ppermute(d_own, "core", SWAP)
    normed, q_raw, k_raw, q, kv, gains, attended, log_total = call(
        attend_kernel,
        [((768, 640), BF), ((4, 256, 256), F32), ((768, 256), F32), ((4, 256, 256), BF), ((768, 512), BF), ((8, 640), F32),
         ((4, 256, 256), BF), ((4, 256, 128), F32)],
        (core, x, x1, x2, q_own, q_oth, cos, sin, place, m5.reshape(1, 640), m2.reshape(1, 256)),
        name="attend",
    )
    f_own, attended = lax.optimization_barrier((f_own, attended))
    f_oth = lax.ppermute(f_own, "core", SWAP)
    mixed, d_hidden, d_att, d_gains, gff_own, gff_oth, gx_own, gx_oth = call(
        feed_kernel,
        [((256, 640), BF), ((256, 640), F32), ((4, 256, 256), BF), ((8, 640), F32)]
        + [((4, 2560, 128), BF)] * 2 + [((128, 80, 128), BF)] * 2,
        (core, x, g, attended, gains, f_own, f_oth, d_own, d_oth),
        name="feed",
    )

    def both(mine, theirs):
        return (mine.astype(F32) + lax.ppermute(theirs.astype(BF), "core", SWAP).astype(F32)).astype(BF)

    gff, gx = (both(gff_own, gff_oth), both(gx_own, gx_oth)[:, :72])
    gx = gx.reshape(4, 2, 2, 2, 4, 72, 128).transpose(1, 3, 0, 2, 4, 5, 6).reshape(4, 32, 72, 128)

    d_q, dkv = call(
        attend_back_kernel,
        [((4, 256, 256), F32), ((768, 512), F32)],
        (q, kv, place, log_total, d_att),
        name="attend_back",
    )
    d_q, dkv, gff, gx = lax.optimization_barrier((d_q, dkv, gff, gx))
    dx0, dx1, dx2, gq_own, gq_oth = call(
        project_back_kernel,
        [((256, 640), F32), ((256, 640), BF), ((256, 640), BF)] + [((4, 1120, 128), BF)] * 2,
        (core, x, x1, x2, normed, q_raw, k_raw, q_own, q_oth, cos, sin, gains, d_gains, m5.reshape(640, 1),
         m2.reshape(256, 1), d_q, dkv, d_hidden),
        name="project_back",
    )
    gq_got = lax.ppermute(gq_oth, "core", SWAP)
    gff_near = lax.psum_scatter(gff, "z")
    gx = lax.all_to_all(gx, Y, 0, 0)
    gq_got, gx, dx1, dx2, gff_near = lax.optimization_barrier((gq_got, gx, dx1, dx2, gff_near))
    gq = (gq_own.astype(F32) + gq_got.astype(F32)).astype(BF)

    def total(back, before, after):
        return back.reshape(before, 2, after, *back.shape[1:]).astype(F32).sum((0, 2))

    gq_near = lax.psum_scatter(gq, "z")
    gx = lax.all_to_all(gx.astype(F32).sum(0).astype(BF), NEAR_Y, 0, 0)
    dx1, dx2 = (along(dx1, -1), along(dx2, -2))
    gx, dx1, dx2, gq_near = lax.optimization_barrier((gx, dx1, dx2, gq_near))
    rest = pieces_of(jnp.concatenate([gff_near, gq_near]), 23, 5)
    rest = lax.all_to_all(rest, NEAR_Z, 0, 0)
    d_x = (dx0 + dx1.astype(F32) + dx2.astype(F32)).astype(BF)
    rest, gx = (total(rest, 2, 8), total(gx, 4, 4))
    grads = [
        whole(rest[:, 80:100], 4, 5, 1024),
        whole(rest[:, 100:105], 1, 5, 256),
        whole(rest[:, 105:110], 1, 5, 256),
        whole(gx[:, 48:72], 3, 8, 640),
        whole(rest[:, :40], 8, 5, 2048),
        whole(rest[:, 40:80], 8, 5, 2048),
        whole(gx[:, :48], 3, 16, 640),
    ]
    at = 0
    for n in GAINS:
        grads.append(rest[0, 110, at : at + n])
        at += n
    return (mixed.reshape(1, 256, 640), d_x.reshape(1, 256, 640), *grads)


def solution(mesh):
    fine = Mesh(mesh.devices.reshape([size for _, size in SIZES]), AXES)
    rows, lines, wide, flat = (P(DP, SEQ, None), P(DP, SEQ), P(AXES, None), P(AXES))
    return jax.shard_map(
        body,
        mesh=fine,
        in_specs=(rows, lines) + (wide,) * 7 + (flat,) * 6 + (rows,),
        out_specs=(rows, rows) + (wide,) * 7 + (flat,) * 6,
        check_vma=False,
    )
```

```python
import functools

import jax
import jax.numpy as jnp
import numpy as np
from jax import lax
from jax.experimental import pallas as pl
from jax.experimental.pallas import tpu as pltpu
from jax.sharding import Mesh, PartitionSpec as P

EPS = 1e-06
BELOW = -1e30
WINDOW = 512
ROOT = 0.7978845608028654
CUBE = 0.044715
SIZES = (("z", 4), ("yh", 2), ("core", 2), ("yl", 2), ("x", 4))
AXES = tuple(name for name, _ in SIZES)
DP, SEQ = (AXES[:3], AXES[3:])
NEAR_Z = ("yh", "core", "yl", "x")
NEAR_Y = ("z", "core", "x")
Y = ("yh", "yl")
SWAP = ((0, 1), (1, 0))
GAINS = (5, 5, 5, 5, 2, 2)
BF, F32 = (jnp.bfloat16, jnp.float32)

ROWS = 160
GATE_AT, UP_AT = (768, 2048)


def dot(a, b):
    return jnp.dot(a, b, preferred_element_type=F32)


def dot_tn(a, b):
    return lax.dot_general(a, b, (((0,), (0,)), ((), ())), preferred_element_type=F32)


def dot_nt(a, b):
    return lax.dot_general(a, b, (((1,), (1,)), ((), ())), preferred_element_type=F32)


def panels(ref, base, count, rows):
    return jnp.concatenate(
        [
            jnp.concatenate([ref[z, pl.ds(base + p * rows, rows), :] for z in range(4)], axis=0)
            for p in range(count)
        ],
        axis=1,
    )


def columns(ref, begin, count):
    return jnp.concatenate([ref[p * 640 : (p + 1) * 640, :] for p in range(begin, begin + count)], axis=1)


def put_panels(ref, base, value, rows):
    for p in range(value.shape[1] // 128):
        for z in range(4):
            ref[z, base + p * rows : base + (p + 1) * rows, :] = value[
                z * rows : (z + 1) * rows, p * 128 : (p + 1) * 128
            ].astype(ref.dtype)


def rms(v, gain):
    return v * lax.rsqrt(jnp.mean(v * v, axis=-1, keepdims=True) + EPS) * (1.0 + gain)


def rms_back(v, gain, dy):
    r = lax.rsqrt(jnp.mean(v * v, axis=-1, keepdims=True) + EPS)
    n = v * r
    dn = dy * (1.0 + gain)
    dv = r * (dn - n * jnp.mean(dn * n, axis=-1, keepdims=True))
    return dv, jnp.sum(dy * n, axis=0, keepdims=True)


def turn(v, c, s):
    a, b = (v[:, :128], v[:, 128:])
    return jnp.concatenate([a * c - b * s, b * c + a * s], axis=1)


def turn_back(d, c, s):
    a, b = (d[:, :128], d[:, 128:])
    return jnp.concatenate([a * c + b * s, b * c - a * s], axis=1)


def owner_mask(width, per):
    d = lax.broadcasted_iota(jnp.int32, (128, width), 0) * per
    j = lax.broadcasted_iota(jnp.int32, (128, width), 1)
    return (j >= d) & (j < d + per)


def allowed_pairs(pos_ref):
    i = lax.broadcasted_iota(jnp.int32, (256, 768), 0)
    j = lax.broadcasted_iota(jnp.int32, (256, 768), 1)
    distance = 512 + i - j
    return (distance >= 0) & (distance <= jnp.minimum(pos_ref[...], WINDOW - 1))


def attend_kernel(
    core_ref, x0, x1, x2, own, oth, table_ref, cos_ref, sin_ref, pos_ref, m5, m2,
    normed_ref, qraw_ref, kraw_ref, q_ref, kv_ref, gain_ref, att_ref, log_ref,
):
    first = core_ref[0] == 0
    table = table_ref[...]
    wide = dot_tn(table, owner_mask(640, 5).astype(BF))
    thin = dot_tn(table, owner_mask(256, 2).astype(BF))
    lane5 = lax.broadcasted_iota(jnp.int32, (128, 640), 0)
    lane2 = lax.broadcasted_iota(jnp.int32, (128, 256), 0)
    gains = [
        jnp.sum(jnp.where(lane5 == m5[...] + 5 * n, wide, 0.0), axis=0, keepdims=True) for n in range(4)
    ]
    heads = [
        jnp.sum(jnp.where(lane2 == m2[...] + 20 + 2 * n, thin, 0.0), axis=0, keepdims=True) for n in range(2)
    ]
    pad = jnp.zeros((1, 384), F32)
    for n in range(4):
        gain_ref[n : n + 1, :] = gains[n]
    for n in range(2):
        gain_ref[4 + n : 5 + n, :] = jnp.concatenate([heads[n], pad], axis=1)
    gain_ref[6:8, :] = jnp.zeros((2, 640), F32)
    for n, ref in enumerate((x2, x1, x0)):
        normed_ref[n * 256 : (n + 1) * 256, :] = rms(ref[...].astype(F32), gains[0]).astype(BF)
    normed = normed_ref[...]
    c, s = (cos_ref[...], sin_ref[...])
    kv_own, kv_oth = [dot(normed, columns(ref, 4, 2)) for ref in (own, oth)]
    left, right = (jnp.where(first, kv_own, kv_oth), jnp.where(first, kv_oth, kv_own))
    kraw = jnp.concatenate([left[:, :128], right[:, :128]], axis=1)
    kraw_ref[...] = kraw
    keys = turn(rms(kraw, heads[1]), c, s).astype(BF)
    values = jnp.concatenate([left[:, 128:], right[:, 128:]], axis=1).astype(BF)
    kv_ref[:, :256] = keys
    kv_ref[:, 256:] = values
    c, s = (c[512:], s[512:])
    allowed = allowed_pairs(pos_ref)
    for side, ref in enumerate((own, oth)):
        raw = dot(normed_ref[512:, :], columns(ref, 0, 4))
        for h in range(2):
            slot = 2 * side + h
            one = raw[:, h * 256 : (h + 1) * 256]
            qraw_ref[slot] = one
            q = turn(rms(one, heads[0]), c, s).astype(BF)
            q_ref[slot] = q
            scores = jnp.where(allowed, dot_nt(q, keys) * 0.0625, BELOW)
            top = jnp.max(scores, axis=-1, keepdims=True)
            exps = jnp.exp(scores - top)
            total = jnp.sum(exps, axis=-1, keepdims=True)
            att_ref[slot] = dot((exps / total).astype(BF), values).astype(BF)
            log_ref[slot] = jnp.broadcast_to(top + jnp.log(total), (256, 128))


def gelu_parts(x):
    t = jnp.tanh(ROOT * (x + CUBE * x * x * x))
    half = 0.5 * (1.0 + t)
    return x * half, half + 0.5 * x * (1.0 - t * t) * ROOT * (1.0 + 3.0 * CUBE * x * x)


def feed_kernel(
    core_ref, x_ref, g_ref, att_ref, gain_ref, own, oth, down_own, down_oth,
    mixed_ref, dhid_ref, datt_ref, dgain_ref, gff_own, gff_oth, gx_own, gx_oth,
):
    core = core_ref[0]
    first = core == 0
    gain_pa, gain_pf, gain_po = [gain_ref[n : n + 1, :] for n in (1, 2, 3)]

    def join(a, b):
        return jnp.where(
            first, jnp.concatenate([a, b[:, 128:]], axis=1), jnp.concatenate([b[:, :256], a], axis=1)
        )

    def part(v):
        low, high = (v[:, :384], v[:, 256:])
        own, oth = (jnp.where(first, low, high), jnp.where(first, high, low))
        lanes = lax.broadcasted_iota(jnp.int32, oth.shape, 1)
        begin = jnp.where(first, 0, 256)
        once = jnp.where((lanes >= begin) & (lanes < begin + 128), 0.0, oth)
        return own.astype(BF), oth.astype(BF), once.astype(BF)

    def out_panels(ref, slot):
        block = lax.rem(slot + 2 * core, 4)
        return jnp.concatenate([ref[block, p * 256 : (p + 1) * 256, :] for p in range(3)], axis=1)

    out_own = [out_panels(own, s) for s in range(4)]
    out_oth = [out_panels(oth, s) for s in range(4)]
    a = sum(dot(att_ref[s], out_own[s]) for s in range(4))
    b = sum(dot(att_ref[s], out_oth[s]) for s in range(4))
    branch = join(a, b)
    hidden = x_ref[...].astype(F32) + rms(branch, gain_pa)
    ff = rms(hidden, gain_pf).astype(BF)

    def down_rows(ref, hand):
        begin = lax.rem(core + hand, 2) * 64
        return jnp.concatenate(
            [ref[pl.ds(begin, 64), p * 16 : (p + 1) * 16].reshape(1024, 128) for p in range(3)], axis=1
        )

    gates = [panels(ref, GATE_AT, 8, ROWS) for ref in (own, oth)]
    ups = [panels(ref, UP_AT, 8, ROWS) for ref in (own, oth)]
    kept = []
    a = b = 0.0
    for hand in range(2):
        gate, up = (dot(ff, gates[hand]), dot(ff, ups[hand]))
        gelu, slope = gelu_parts(gate)
        product = (gelu * up).astype(BF)
        kept.append((up * slope, gelu, product))
        a = a + dot(product, down_rows(down_own, hand))
        b = b + dot(product, down_rows(down_oth, hand))
    ff_out = join(a, b)
    mixed_ref[...] = (hidden + rms(ff_out, gain_po)).astype(BF)

    g = g_ref[...].astype(F32)
    d_ff_out, d_po = rms_back(ff_out, gain_po, g)
    d_own, d_oth, d_oth_once = part(d_ff_out)
    d_in = 0.0
    for hand in range(2):
        slope, gelu, product = kept[hand]
        for ref, d in ((gx_own, d_own), (gx_oth, d_oth)):
            grad = dot_tn(product, d).astype(BF)
            for p in range(3):
                cut = grad[:, p * 128 : (p + 1) * 128].reshape(2, 2, 2, 2, 4, 16, 128)
                for z, yh, c, yl in np.ndindex(2, 2, 2, 2):
                    at = (2 * lax.rem(core + hand, 2) + z) * 8 + c * 4
                    ref[2 * yh + yl, pl.ds(at, 4), p * 16 : (p + 1) * 16] = cut[z, yh, c, yl]
        d_product = dot_nt(d_own, down_rows(down_own, hand)) + dot_nt(d_oth_once, down_rows(down_oth, hand))
        d_gate, d_up = ((d_product * slope).astype(BF), (d_product * gelu).astype(BF))
        ref = (gff_own, gff_oth)[hand]
        put_panels(ref, 0, dot_tn(ff, d_gate), ROWS)
        put_panels(ref, UP_AT - GATE_AT, dot_tn(ff, d_up), ROWS)
        d_in = d_in + dot_nt(d_gate, gates[hand]) + dot_nt(d_up, ups[hand])
    d_hidden, d_pf = rms_back(hidden, gain_pf, d_in)
    d_hidden = d_hidden + g
    dhid_ref[...] = d_hidden
    d_branch, d_pa = rms_back(branch, gain_pa, d_hidden)
    d_own, d_oth, d_oth_once = part(d_branch)
    for s in range(4):
        block = lax.rem(s + 2 * core, 4)
        for ref, d in ((gx_own, d_own), (gx_oth, d_oth)):
            grad = dot_tn(att_ref[s], d)
            cut = [grad[:, p * 128 : (p + 1) * 128].reshape(32, 8, 128) for p in range(3)]
            cut.append(jnp.zeros_like(cut[0]))
            for pair in range(2):
                rows = jnp.concatenate(cut[2 * pair : 2 * pair + 2], axis=1).astype(BF)
                rows = rows.reshape(2, 2, 2, 4, 16, 128)
                for yh, c, yl in np.ndindex(2, 2, 2):
                    at = block * 8 + c * 4
                    ref[2 * yh + yl, pl.ds(at, 4), 48 + pair * 16 : 64 + pair * 16] = rows[yh, c, yl]
        datt_ref[s] = (dot_nt(d_own, out_own[s]) + dot_nt(d_oth_once, out_oth[s])).astype(BF)
    dgain_ref[0:1, :] = d_pa
    dgain_ref[1:2, :] = d_pf
    dgain_ref[2:3, :] = d_po
    dgain_ref[3:8, :] = jnp.zeros((5, 640), F32)


def attend_back_kernel(q_ref, kv_ref, pos_ref, log_ref, datt_ref, dq_ref, dkv_ref):
    keys, values = (kv_ref[:, :256], kv_ref[:, 256:])
    allowed = allowed_pairs(pos_ref)
    dk = dv = 0.0
    for h in range(4):
        q, d_att = (q_ref[h], datt_ref[h])
        scores = jnp.where(allowed, dot_nt(q, keys) * 0.0625, BELOW)
        probs = jnp.exp(scores - log_ref[h][:, :1])
        dv = dv + dot_tn(probs.astype(BF), d_att)
        d_probs = dot_nt(d_att, values)
        inner = jnp.sum(probs * d_probs, axis=-1, keepdims=True)
        d_scores = (probs * (d_probs - inner) * 0.0625).astype(BF)
        dk = dk + dot_tn(d_scores, q)
        dq_ref[h] = dot(d_scores, keys)
    dkv_ref[:, :256] = dk
    dkv_ref[:, 256:] = dv


def project_back_kernel(
    core_ref, x0, x1, x2, normed_ref, qraw_ref, kraw_ref, own, oth, cos_ref, sin_ref, gain_ref, dgain_ref, c5, c2,
    dq_ref, dkv_ref, dhid_ref, dx0, dx1, dx2, g_own, g_oth,
):
    first = core_ref[0] == 0
    c, s = (cos_ref[...], sin_ref[...])
    gain_q, gain_k = (gain_ref[4:5, :256], gain_ref[5:6, :256])
    dk, dv = (dkv_ref[:, :256], dkv_ref[:, 256:])
    d_gain_q = 0.0
    d_qs = []
    for h in range(4):
        d, dg = rms_back(qraw_ref[h], gain_q, turn_back(dq_ref[h], c[512:], s[512:]))
        d_gain_q = d_gain_q + dg
        d_qs.append(d.astype(BF))
    d_k, d_gain_k = rms_back(kraw_ref[...], gain_k, turn_back(dk, c, s))
    left = jnp.concatenate([d_k[:, :128], dv[:, :128]], axis=1)
    right = jnp.concatenate([d_k[:, 128:], dv[:, 128:]], axis=1)
    sides = (jnp.where(first, left, right).astype(BF), jnp.where(first, right, left).astype(BF))
    d_query = d_normed = 0.0
    for side, (w, ref) in enumerate(((own, g_own), (oth, g_oth))):
        d_q = jnp.concatenate(d_qs[2 * side : 2 * side + 2], axis=1)
        put_panels(ref, 0, dot_tn(normed_ref[512:, :], d_q), ROWS)
        put_panels(ref, 4 * ROWS, dot_tn(normed_ref[...], sides[side]), ROWS)
        d_query = d_query + dot_nt(d_q, columns(w, 0, 4))
        d_normed = d_normed + dot_nt(sides[side], columns(w, 4, 2))
    d_in = 0.0
    for n, (x_ref, out) in enumerate(((x2, dx2), (x1, dx1), (x0, dx0))):
        d = d_normed[n * 256 : (n + 1) * 256]
        if n == 2:
            d = d + d_query
        dx, dg = rms_back(x_ref[...].astype(F32), gain_ref[0:1, :], d)
        d_in = d_in + dg
        out[...] = (dx + dhid_ref[...] if n == 2 else dx).astype(out.dtype)
    mask5, mask2 = (owner_mask(640, 5), owner_mask(256, 2))
    lane5 = lax.broadcasted_iota(jnp.int32, (640, 128), 1)
    lane2 = lax.broadcasted_iota(jnp.int32, (256, 128), 1)
    table = 0.0
    for n, d in enumerate((d_in, dgain_ref[0:1, :], dgain_ref[1:2, :], dgain_ref[2:3, :])):
        place = (lane5 == c5[...] + 5 * n).astype(F32).astype(BF)
        table = table + dot(jnp.where(mask5, d, 0.0).astype(BF), place)
    for n, d in enumerate((d_gain_q, d_gain_k)):
        place = (lane2 == c2[...] + 20 + 2 * n).astype(F32).astype(BF)
        table = table + dot(jnp.where(mask2, d, 0.0).astype(BF), place)
    feature = lax.broadcasted_iota(jnp.int32, (640, 128), 0)
    owner = lax.broadcasted_iota(jnp.int32, (640, 128), 1)
    table = dot((feature == 5 * owner).astype(F32).astype(BF), table.astype(BF))
    for ref in (g_own, g_oth):
        put_panels(ref, 6 * ROWS, table, ROWS)


def finish_kernel(rest_ref, gx_ref, wq, wk, wv, wout, wgate, wup, wdown, *others):
    *gains, rest, gx = others
    for core in range(2):
        rest[core, 112:, :] = jnp.zeros((8, 128), F32)
        for ref, total, after in ((rest_ref, rest, 8), (gx_ref, gx, 4)):
            acc = 0.0
            for i in range(32):
                if i // after % 2 == core:
                    acc = acc + ref[i].astype(F32)
            total[core, : acc.shape[0], :] = acc
    for out, begin, count in ((wgate, 0, 8), (wup, 40, 8), (wq, 80, 4), (wk, 100, 1), (wv, 105, 1)):
        for core in range(2):
            for p in range(count):
                at = (core * count + p) * 128
                out[:, at : at + 128] = rest[core, begin + p * 5 : begin + p * 5 + 5, :]
    for out, begin, rows in ((wdown, 0, 16), (wout, 48, 8)):
        for n, (core, p) in enumerate(((0, 0), (0, 1), (1, 0), (1, 1), (1, 2))):
            out[:, n * 128 : (n + 1) * 128] = gx[core, begin + p * rows : begin + (p + 1) * rows, :]
    at = 0
    for ref, n in zip(gains, GAINS):
        ref[...] = rest[0, 110:111, at : at + n]
        at += n


def call(kernel, outs, args, scratch=(), name=None):
    vmem = pl.BlockSpec(memory_space=pltpu.VMEM)
    smem = pl.BlockSpec(memory_space=pltpu.SMEM)
    return pl.pallas_call(
        kernel,
        out_shape=[jax.ShapeDtypeStruct(shape, dtype) for shape, dtype in outs],
        in_specs=[smem if a.shape == (1,) else vmem for a in args],
        out_specs=[vmem] * len(outs),
        scratch_shapes=list(scratch),
        compiler_params=pltpu.CompilerParams(vmem_limit_bytes=60 * 1024 * 1024),
        name=name,
    )(*args)


def halves(a):
    rows, width = a.shape
    if width % 256:
        cut = a.reshape(rows, -1, 128).transpose(1, 0, 2)
        part = (width + 128) // 256
        return jnp.stack([cut[:part], cut[-part:]]).reshape(2, -1, 128)
    return a.reshape(rows, 2, -1, 128).transpose(1, 2, 0, 3).reshape(2, -1, 128)


def to_all(flat, before, after):
    wide = jnp.broadcast_to(flat[None, :, None], (before, 2, after, *flat.shape[1:]))
    return wide.reshape(-1, *flat.shape[1:])


def block_of(near, at, panel_count, rows):
    cut = near[:, at : at + panel_count * rows].reshape(-1, panel_count, rows, 128)
    return cut.transpose(1, 0, 2, 3).reshape(-1, 128)


def pieces_of(block, panel_count, rows):
    cut = block.reshape(panel_count, -1, rows, 128)
    return cut.transpose(1, 0, 2, 3).reshape(cut.shape[1], -1, 128)


def body(
    tokens, positions, w_query, w_key, w_value, w_out, w_gate, w_up, w_down,
    norm_input, norm_post_attn, norm_pre_ff, norm_post_ff, norm_query, norm_key, cotangent,
):
    core = lax.axis_index("core").astype(jnp.int32).reshape(1)
    x = tokens.reshape(256, 640)
    g = cotangent.reshape(256, 640)

    def along(v, distance):
        return lax.ppermute(v, SEQ, [(i - distance, i) for i in range(8) if 0 <= i - distance < 8])

    x1, x2 = (along(x, 1), along(x, 2))
    place = positions.reshape(256, 1)
    before = positions[:, :1] - jnp.arange(512, 0, -1, dtype=jnp.int32)[None]
    places = jnp.concatenate([before, positions], axis=1).reshape(768, 1)
    steps = jnp.arange(128).astype(F32)
    angles = places.astype(F32) * (10000.0 ** (-2.0 * steps / 256))
    cos, sin = (jnp.cos(angles), jnp.sin(angles))
    m5, m2 = [jnp.asarray((np.arange(n) % k).astype(np.int32)) for n, k in ((640, 5), (256, 2))]

    gain_row = jnp.concatenate([norm_input, norm_post_attn, norm_pre_ff, norm_post_ff, norm_query, norm_key])
    gain_row = jnp.pad(gain_row, (0, 104)).reshape(1, 1, 128)
    flat = jnp.concatenate(
        [halves(w_query), halves(w_key), halves(w_value), jnp.broadcast_to(gain_row, (2, 1, 128))], axis=1
    )
    flat_ff = jnp.concatenate([halves(w_out), halves(w_gate), halves(w_up)], axis=1)
    near = lax.all_to_all(to_all(flat_ff, 2, 8), NEAR_Z, 0, 0)
    flat = jnp.concatenate([halves(w_down), flat], axis=1)
    near, flat, cos, sin, place = lax.optimization_barrier((near, flat, cos, sin, place))
    block = jnp.concatenate([block_of(near, 0, 3, 8), block_of(near, 24, 8, 5), block_of(near, 64, 8, 5)])
    f_own = lax.all_gather(block, "z")

    near = lax.all_to_all(to_all(flat, 8, 8), AXES, 0, 0)
    q_own, table = (block_of(near, 48, 6, 5), near[:, 78])
    q_own, x1, x2 = lax.optimization_barrier((q_own, x1, x2))
    q_oth = lax.ppermute(q_own, "core", SWAP)
    d_own = near[:, :48]
    d_oth = lax.ppermute(d_own, "core", SWAP)
    normed, q_raw, k_raw, q, kv, gains, attended, log_total = call(
        attend_kernel,
        [((768, 640), BF), ((4, 256, 256), F32), ((768, 256), F32), ((4, 256, 256), BF), ((768, 512), BF), ((8, 640), F32),
         ((4, 256, 256), BF), ((4, 256, 128), F32)],
        (core, x, x1, x2, q_own, q_oth, table, cos, sin, place, m5.reshape(1, 640), m2.reshape(1, 256)),
        name="attend",
    )
    f_own, attended = lax.optimization_barrier((f_own, attended))
    f_oth = lax.ppermute(f_own, "core", SWAP)
    mixed, d_hidden, d_att, d_gains, gff_own, gff_oth, gx_own, gx_oth = call(
        feed_kernel,
        [((256, 640), BF), ((256, 640), F32), ((4, 256, 256), BF), ((8, 640), F32)]
        + [((4, 2560, 128), BF)] * 2 + [((4, 32, 80, 128), BF)] * 2,
        (core, x, g, attended, gains, f_own, f_oth, d_own, d_oth),
        name="feed",
    )

    def both(mine, theirs):
        return (mine.astype(F32) + lax.ppermute(theirs.astype(BF), "core", SWAP).astype(F32)).astype(BF)

    gff, gx = (both(gff_own, gff_oth), both(gx_own, gx_oth)[:, :, :72])

    d_att, gff, gx = lax.optimization_barrier((d_att, gff, gx))
    d_q, dkv = call(
        attend_back_kernel,
        [((4, 256, 256), F32), ((768, 512), F32)],
        (q, kv, place, log_total, d_att),
        name="attend_back",
    )
    dx0, dx1, dx2, gq_own, gq_oth = call(
        project_back_kernel,
        [((256, 640), F32), ((256, 640), BF), ((256, 640), BF)] + [((4, 1120, 128), BF)] * 2,
        (core, x, x1, x2, normed, q_raw, k_raw, q_own, q_oth, cos, sin, gains, d_gains, m5.reshape(640, 1),
         m2.reshape(256, 1), d_q, dkv, d_hidden),
        name="project_back",
    )
    gq_got = lax.ppermute(gq_oth, "core", SWAP)
    gff_near = lax.psum_scatter(gff, "z")
    gx = lax.all_to_all(gx, Y, 0, 0)
    gq_got, gx, dx1, dx2, gff_near = lax.optimization_barrier((gq_got, gx, dx1, dx2, gff_near))
    gq = (gq_own.astype(F32) + gq_got.astype(F32)).astype(BF)

    gq_near = lax.psum_scatter(gq, "z")
    gx = lax.all_to_all(gx.astype(F32).sum(0).astype(BF), NEAR_Y, 0, 0)
    dx1, dx2 = (along(dx1, -1), along(dx2, -2))
    ff = pieces_of(gff_near, 16, 5)
    gx, dx1, dx2, ff, gq_near = lax.optimization_barrier((gx, dx1, dx2, ff, gq_near))
    rest = lax.all_to_all(jnp.concatenate([ff, pieces_of(gq_near, 7, 5)], axis=1), NEAR_Z, 0, 0)
    d_x = (dx0 + dx1.astype(F32) + dx2.astype(F32)).astype(BF)
    grads = call(
        finish_kernel,
        [((5, 1024), F32), ((5, 256), F32), ((5, 256), F32), ((8, 640), F32), ((5, 2048), F32), ((5, 2048), F32),
         ((16, 640), F32)] + [((1, n), F32) for n in GAINS],
        (rest, gx),
        scratch=(pltpu.VMEM((2, 120, 128), F32), pltpu.VMEM((2, 72, 128), F32)),
        name="finish",
    )
    grads = [g.reshape(-1) if g.shape[0] == 1 else g for g in grads]
    return (mixed.reshape(1, 256, 640), d_x.reshape(1, 256, 640), *grads)


def solution(mesh):
    fine = Mesh(mesh.devices.reshape([size for _, size in SIZES]), AXES)
    rows, lines, wide, flat = (P(DP, SEQ, None), P(DP, SEQ), P(AXES, None), P(AXES))
    return jax.shard_map(
        body,
        mesh=fine,
        in_specs=(rows, lines) + (wide,) * 7 + (flat,) * 6 + (rows,),
        out_specs=(rows, rows) + (wide,) * 7 + (flat,) * 6,
        check_vma=False,
    )
```

```python
import functools

import jax
import jax.numpy as jnp
import numpy as np
from jax import lax
from jax.experimental import pallas as pl
from jax.experimental.pallas import tpu as pltpu
from jax.sharding import Mesh, PartitionSpec as P

EPS = 1e-06
BELOW = -1e30
WINDOW = 512
ROOT = 0.7978845608028654
CUBE = 0.044715
SIZES = (("z", 4), ("yh", 2), ("core", 2), ("yl", 2), ("x", 4))
AXES = tuple(name for name, _ in SIZES)
DP, SEQ = (AXES[:3], AXES[3:])
NEAR_Z = ("yh", "core", "yl", "x")
NEAR_Y = ("z", "core", "x")
Y = ("yh", "yl")
SWAP = ((0, 1), (1, 0))
GAINS = (5, 5, 5, 5, 2, 2)
BF, F32 = (jnp.bfloat16, jnp.float32)

ROWS = 160
GATE_AT, UP_AT = (768, 2048)


def dot(a, b):
    return jnp.dot(a, b, preferred_element_type=F32)


def dot_tn(a, b):
    return lax.dot_general(a, b, (((0,), (0,)), ((), ())), preferred_element_type=F32)


def dot_nt(a, b):
    return lax.dot_general(a, b, (((1,), (1,)), ((), ())), preferred_element_type=F32)


def panels(ref, base, count, rows):
    return jnp.concatenate(
        [
            jnp.concatenate([ref[z, pl.ds(base + p * rows, rows), :] for z in range(4)], axis=0)
            for p in range(count)
        ],
        axis=1,
    )


def columns(ref, begin, count):
    return jnp.concatenate([ref[p * 640 : (p + 1) * 640, :] for p in range(begin, begin + count)], axis=1)


def put_panels(ref, base, value, rows):
    for p in range(value.shape[1] // 128):
        for z in range(4):
            ref[z, base + p * rows : base + (p + 1) * rows, :] = value[
                z * rows : (z + 1) * rows, p * 128 : (p + 1) * 128
            ].astype(ref.dtype)


def rms(v, gain):
    return v * lax.rsqrt(jnp.mean(v * v, axis=-1, keepdims=True) + EPS) * (1.0 + gain)


def rms_back(v, gain, dy):
    r = lax.rsqrt(jnp.mean(v * v, axis=-1, keepdims=True) + EPS)
    n = v * r
    dn = dy * (1.0 + gain)
    dv = r * (dn - n * jnp.mean(dn * n, axis=-1, keepdims=True))
    return dv, jnp.sum(dy * n, axis=0, keepdims=True)


def turn(v, c, s):
    a, b = (v[:, :128], v[:, 128:])
    return jnp.concatenate([a * c - b * s, b * c + a * s], axis=1)


def turn_back(d, c, s):
    a, b = (d[:, :128], d[:, 128:])
    return jnp.concatenate([a * c + b * s, b * c - a * s], axis=1)


def owner_mask(width, per):
    d = lax.broadcasted_iota(jnp.int32, (128, width), 0) * per
    j = lax.broadcasted_iota(jnp.int32, (128, width), 1)
    return (j >= d) & (j < d + per)


def allowed_pairs(pos_ref):
    i = lax.broadcasted_iota(jnp.int32, (256, 768), 0)
    j = lax.broadcasted_iota(jnp.int32, (256, 768), 1)
    distance = 512 + i - j
    return (distance >= 0) & (distance <= jnp.minimum(pos_ref[...], WINDOW - 1))


def attend_kernel(
    core_ref, x0, x1, x2, own, oth, table_ref, cos_ref, sin_ref, pos_ref, m5, m2,
    normed_ref, qraw_ref, kraw_ref, q_ref, kv_ref, gain_ref, att_ref, log_ref,
):
    first = core_ref[0] == 0
    table = table_ref[...]
    wide = dot_tn(table, owner_mask(640, 5).astype(BF))
    thin = dot_tn(table, owner_mask(256, 2).astype(BF))
    lane5 = lax.broadcasted_iota(jnp.int32, (128, 640), 0)
    lane2 = lax.broadcasted_iota(jnp.int32, (128, 256), 0)
    gains = [
        jnp.sum(jnp.where(lane5 == m5[...] + 5 * n, wide, 0.0), axis=0, keepdims=True) for n in range(4)
    ]
    heads = [
        jnp.sum(jnp.where(lane2 == m2[...] + 20 + 2 * n, thin, 0.0), axis=0, keepdims=True) for n in range(2)
    ]
    pad = jnp.zeros((1, 384), F32)
    for n in range(4):
        gain_ref[n : n + 1, :] = gains[n]
    for n in range(2):
        gain_ref[4 + n : 5 + n, :] = jnp.concatenate([heads[n], pad], axis=1)
    gain_ref[6:8, :] = jnp.zeros((2, 640), F32)
    for n, ref in enumerate((x2, x1, x0)):
        normed_ref[n * 256 : (n + 1) * 256, :] = rms(ref[...].astype(F32), gains[0]).astype(BF)
    normed = normed_ref[...]
    c, s = (cos_ref[...], sin_ref[...])
    kv_own, kv_oth = [dot(normed, columns(ref, 4, 2)) for ref in (own, oth)]
    left, right = (jnp.where(first, kv_own, kv_oth), jnp.where(first, kv_oth, kv_own))
    kraw = jnp.concatenate([left[:, :128], right[:, :128]], axis=1)
    kraw_ref[...] = kraw
    keys = turn(rms(kraw, heads[1]), c, s).astype(BF)
    values = jnp.concatenate([left[:, 128:], right[:, 128:]], axis=1).astype(BF)
    kv_ref[:, :256] = keys
    kv_ref[:, 256:] = values
    c, s = (c[512:], s[512:])
    allowed = allowed_pairs(pos_ref)
    for side, ref in enumerate((own, oth)):
        raw = dot(normed_ref[512:, :], columns(ref, 0, 4))
        for h in range(2):
            slot = 2 * side + h
            one = raw[:, h * 256 : (h + 1) * 256]
            qraw_ref[slot] = one
            q = turn(rms(one, heads[0]), c, s).astype(BF)
            q_ref[slot] = q
            scores = jnp.where(allowed, dot_nt(q, keys) * 0.0625, BELOW)
            top = jnp.max(scores, axis=-1, keepdims=True)
            exps = jnp.exp(scores - top)
            total = jnp.sum(exps, axis=-1, keepdims=True)
            att_ref[slot] = dot((exps / total).astype(BF), values).astype(BF)
            log_ref[slot] = jnp.broadcast_to(top + jnp.log(total), (256, 128))


def gelu_parts(x):
    t = jnp.tanh(ROOT * (x + CUBE * x * x * x))
    half = 0.5 * (1.0 + t)
    return x * half, half + 0.5 * x * (1.0 - t * t) * ROOT * (1.0 + 3.0 * CUBE * x * x)


def feed_kernel(
    core_ref, x_ref, g_ref, att_ref, gain_ref, own, oth, down_own, down_oth,
    mixed_ref, dhid_ref, datt_ref, dgain_ref, gff_own, gff_oth, gx_own, gx_oth,
):
    core = core_ref[0]
    first = core == 0
    gain_pa, gain_pf, gain_po = [gain_ref[n : n + 1, :] for n in (1, 2, 3)]

    def join(a, b):
        return jnp.where(
            first, jnp.concatenate([a, b[:, 128:]], axis=1), jnp.concatenate([b[:, :256], a], axis=1)
        )

    def part(v):
        low, high = (v[:, :384], v[:, 256:])
        own, oth = (jnp.where(first, low, high), jnp.where(first, high, low))
        lanes = lax.broadcasted_iota(jnp.int32, oth.shape, 1)
        begin = jnp.where(first, 0, 256)
        once = jnp.where((lanes >= begin) & (lanes < begin + 128), 0.0, oth)
        return own.astype(BF), oth.astype(BF), once.astype(BF)

    def out_panels(ref, slot):
        block = lax.rem(slot + 2 * core, 4)
        return jnp.concatenate([ref[block, p * 256 : (p + 1) * 256, :] for p in range(3)], axis=1)

    out_own = [out_panels(own, s) for s in range(4)]
    out_oth = [out_panels(oth, s) for s in range(4)]
    a = sum(dot(att_ref[s], out_own[s]) for s in range(4))
    b = sum(dot(att_ref[s], out_oth[s]) for s in range(4))
    branch = join(a, b)
    hidden = x_ref[...].astype(F32) + rms(branch, gain_pa)
    ff = rms(hidden, gain_pf).astype(BF)

    def down_rows(ref, hand):
        begin = lax.rem(core + hand, 2) * 64
        return jnp.concatenate(
            [ref[pl.ds(begin, 64), p * 16 : (p + 1) * 16].reshape(1024, 128) for p in range(3)], axis=1
        )

    gates = [panels(ref, GATE_AT, 8, ROWS) for ref in (own, oth)]
    ups = [panels(ref, UP_AT, 8, ROWS) for ref in (own, oth)]
    kept = []
    a = b = 0.0
    for hand in range(2):
        gate, up = (dot(ff, gates[hand]), dot(ff, ups[hand]))
        gelu, slope = gelu_parts(gate)
        product = (gelu * up).astype(BF)
        kept.append((up * slope, gelu, product))
        a = a + dot(product, down_rows(down_own, hand))
        b = b + dot(product, down_rows(down_oth, hand))
    ff_out = join(a, b)
    mixed_ref[...] = (hidden + rms(ff_out, gain_po)).astype(BF)

    g = g_ref[...].astype(F32)
    d_ff_out, d_po = rms_back(ff_out, gain_po, g)
    d_own, d_oth, d_oth_once = part(d_ff_out)
    d_in = 0.0
    for hand in range(2):
        slope, gelu, product = kept[hand]
        for ref, d in ((gx_own, d_own), (gx_oth, d_oth)):
            grad = dot_tn(product, d).astype(BF)
            for p in range(3):
                cut = grad[:, p * 128 : (p + 1) * 128].reshape(2, 2, 2, 2, 4, 16, 128)
                for z, yh, c, yl in np.ndindex(2, 2, 2, 2):
                    at = (2 * lax.rem(core + hand, 2) + z) * 8 + c * 4
                    ref[2 * yh + yl, pl.ds(at, 4), p * 16 : (p + 1) * 16] = cut[z, yh, c, yl]
        d_product = dot_nt(d_own, down_rows(down_own, hand)) + dot_nt(d_oth_once, down_rows(down_oth, hand))
        d_gate, d_up = ((d_product * slope).astype(BF), (d_product * gelu).astype(BF))
        ref = (gff_own, gff_oth)[hand]
        put_panels(ref, 0, dot_tn(ff, d_gate), ROWS)
        put_panels(ref, UP_AT - GATE_AT, dot_tn(ff, d_up), ROWS)
        d_in = d_in + dot_nt(d_gate, gates[hand]) + dot_nt(d_up, ups[hand])
    d_hidden, d_pf = rms_back(hidden, gain_pf, d_in)
    d_hidden = d_hidden + g
    dhid_ref[...] = d_hidden
    d_branch, d_pa = rms_back(branch, gain_pa, d_hidden)
    d_own, d_oth, d_oth_once = part(d_branch)
    for s in range(4):
        block = lax.rem(s + 2 * core, 4)
        for ref, d in ((gx_own, d_own), (gx_oth, d_oth)):
            grad = dot_tn(att_ref[s], d)
            cut = [grad[:, p * 128 : (p + 1) * 128].reshape(32, 8, 128) for p in range(3)]
            cut.append(jnp.zeros_like(cut[0]))
            for pair in range(2):
                rows = jnp.concatenate(cut[2 * pair : 2 * pair + 2], axis=1).astype(BF)
                rows = rows.reshape(2, 2, 2, 4, 16, 128)
                for yh, c, yl in np.ndindex(2, 2, 2):
                    at = block * 8 + c * 4
                    ref[2 * yh + yl, pl.ds(at, 4), 48 + pair * 16 : 64 + pair * 16] = rows[yh, c, yl]
        datt_ref[s] = (dot_nt(d_own, out_own[s]) + dot_nt(d_oth_once, out_oth[s])).astype(BF)
    dgain_ref[0:1, :] = d_pa
    dgain_ref[1:2, :] = d_pf
    dgain_ref[2:3, :] = d_po
    dgain_ref[3:8, :] = jnp.zeros((5, 640), F32)


def attend_back_kernel(q_ref, kv_ref, pos_ref, log_ref, datt_ref, dq_ref, dkv_ref):
    keys, values = (kv_ref[:, :256], kv_ref[:, 256:])
    allowed = allowed_pairs(pos_ref)
    dk = dv = 0.0
    for h in range(4):
        q, d_att = (q_ref[h], datt_ref[h])
        scores = jnp.where(allowed, dot_nt(q, keys) * 0.0625, BELOW)
        probs = jnp.exp(scores - log_ref[h][:, :1])
        dv = dv + dot_tn(probs.astype(BF), d_att)
        d_probs = dot_nt(d_att, values)
        inner = jnp.sum(probs * d_probs, axis=-1, keepdims=True)
        d_scores = (probs * (d_probs - inner) * 0.0625).astype(BF)
        dk = dk + dot_tn(d_scores, q)
        dq_ref[h] = dot(d_scores, keys)
    dkv_ref[:, :256] = dk
    dkv_ref[:, 256:] = dv


def project_back_kernel(
    core_ref, x0, x1, x2, normed_ref, qraw_ref, kraw_ref, own, oth, cos_ref, sin_ref, gain_ref, dgain_ref, c5, c2,
    dq_ref, dkv_ref, dhid_ref, dx0, dx1, dx2, g_own, g_oth,
):
    first = core_ref[0] == 0
    c, s = (cos_ref[...], sin_ref[...])
    gain_q, gain_k = (gain_ref[4:5, :256], gain_ref[5:6, :256])
    dk, dv = (dkv_ref[:, :256], dkv_ref[:, 256:])
    d_gain_q = 0.0
    d_qs = []
    for h in range(4):
        d, dg = rms_back(qraw_ref[h], gain_q, turn_back(dq_ref[h], c[512:], s[512:]))
        d_gain_q = d_gain_q + dg
        d_qs.append(d.astype(BF))
    d_k, d_gain_k = rms_back(kraw_ref[...], gain_k, turn_back(dk, c, s))
    left = jnp.concatenate([d_k[:, :128], dv[:, :128]], axis=1)
    right = jnp.concatenate([d_k[:, 128:], dv[:, 128:]], axis=1)
    sides = (jnp.where(first, left, right).astype(BF), jnp.where(first, right, left).astype(BF))
    d_query = d_normed = 0.0
    for side, (w, ref) in enumerate(((own, g_own), (oth, g_oth))):
        d_q = jnp.concatenate(d_qs[2 * side : 2 * side + 2], axis=1)
        put_panels(ref, 0, dot_tn(normed_ref[512:, :], d_q), ROWS)
        put_panels(ref, 4 * ROWS, dot_tn(normed_ref[...], sides[side]), ROWS)
        d_query = d_query + dot_nt(d_q, columns(w, 0, 4))
        d_normed = d_normed + dot_nt(sides[side], columns(w, 4, 2))
    d_in = 0.0
    for n, (x_ref, out) in enumerate(((x2, dx2), (x1, dx1), (x0, dx0))):
        d = d_normed[n * 256 : (n + 1) * 256]
        if n == 2:
            d = d + d_query
        dx, dg = rms_back(x_ref[...].astype(F32), gain_ref[0:1, :], d)
        d_in = d_in + dg
        out[...] = (dx + dhid_ref[...] if n == 2 else dx).astype(out.dtype)
    mask5, mask2 = (owner_mask(640, 5), owner_mask(256, 2))
    lane5 = lax.broadcasted_iota(jnp.int32, (640, 128), 1)
    lane2 = lax.broadcasted_iota(jnp.int32, (256, 128), 1)
    table = 0.0
    for n, d in enumerate((d_in, dgain_ref[0:1, :], dgain_ref[1:2, :], dgain_ref[2:3, :])):
        place = (lane5 == c5[...] + 5 * n).astype(F32).astype(BF)
        table = table + dot(jnp.where(mask5, d, 0.0).astype(BF), place)
    for n, d in enumerate((d_gain_q, d_gain_k)):
        place = (lane2 == c2[...] + 20 + 2 * n).astype(F32).astype(BF)
        table = table + dot(jnp.where(mask2, d, 0.0).astype(BF), place)
    feature = lax.broadcasted_iota(jnp.int32, (640, 128), 0)
    owner = lax.broadcasted_iota(jnp.int32, (640, 128), 1)
    table = dot((feature == 5 * owner).astype(F32).astype(BF), table.astype(BF))
    for ref in (g_own, g_oth):
        put_panels(ref, 6 * ROWS, table, ROWS)


def finish_kernel(rest_ref, gx_ref, wq, wk, wv, wout, wgate, wup, wdown, *others):
    *gains, rest, gx = others
    for core in range(2):
        rest[core, 112:, :] = jnp.zeros((8, 128), F32)
        for ref, total, after in ((rest_ref, rest, 8), (gx_ref, gx, 4)):
            acc = 0.0
            for i in range(32):
                if i // after % 2 == core:
                    acc = acc + ref[i].astype(F32)
            total[core, : acc.shape[0], :] = acc
    for out, begin, count in ((wgate, 0, 8), (wup, 40, 8), (wq, 80, 4), (wk, 100, 1), (wv, 105, 1)):
        for core in range(2):
            for p in range(count):
                at = (core * count + p) * 128
                out[:, at : at + 128] = rest[core, begin + p * 5 : begin + p * 5 + 5, :]
    for out, begin, rows in ((wdown, 0, 16), (wout, 48, 8)):
        for n, (core, p) in enumerate(((0, 0), (0, 1), (1, 0), (1, 1), (1, 2))):
            out[:, n * 128 : (n + 1) * 128] = gx[core, begin + p * rows : begin + (p + 1) * rows, :]
    at = 0
    for ref, n in zip(gains, GAINS):
        ref[...] = rest[0, 110:111, at : at + n]
        at += n


def call(kernel, outs, args, scratch=(), name=None):
    vmem = pl.BlockSpec(memory_space=pltpu.VMEM)
    smem = pl.BlockSpec(memory_space=pltpu.SMEM)
    return pl.pallas_call(
        kernel,
        out_shape=[jax.ShapeDtypeStruct(shape, dtype) for shape, dtype in outs],
        in_specs=[smem if a.shape == (1,) else vmem for a in args],
        out_specs=[vmem] * len(outs),
        scratch_shapes=list(scratch),
        compiler_params=pltpu.CompilerParams(vmem_limit_bytes=60 * 1024 * 1024),
        name=name,
    )(*args)


def halves(a):
    rows, width = a.shape
    if width % 256:
        cut = a.reshape(rows, -1, 128).transpose(1, 0, 2)
        part = (width + 128) // 256
        return jnp.stack([cut[:part], cut[-part:]]).reshape(2, -1, 128)
    return a.reshape(rows, 2, -1, 128).transpose(1, 2, 0, 3).reshape(2, -1, 128)


def to_all(flat, before, after):
    wide = jnp.broadcast_to(flat[None, :, None], (before, 2, after, *flat.shape[1:]))
    return wide.reshape(-1, *flat.shape[1:])


def block_of(near, at, panel_count, rows):
    cut = near[:, at : at + panel_count * rows].reshape(-1, panel_count, rows, 128)
    return cut.transpose(1, 0, 2, 3).reshape(-1, 128)


def pieces_of(block, panel_count, rows):
    cut = block.reshape(panel_count, -1, rows, 128)
    return cut.transpose(1, 0, 2, 3).reshape(cut.shape[1], -1, 128)


def body(
    tokens, positions, w_query, w_key, w_value, w_out, w_gate, w_up, w_down,
    norm_input, norm_post_attn, norm_pre_ff, norm_post_ff, norm_query, norm_key, cotangent,
):
    core = lax.axis_index("core").astype(jnp.int32).reshape(1)
    x = tokens.reshape(256, 640)
    g = cotangent.reshape(256, 640)

    def along(v, distance):
        return lax.ppermute(v, SEQ, [(i - distance, i) for i in range(8) if 0 <= i - distance < 8])

    x1, x2 = (along(x, 1), along(x, 2))
    place = positions.reshape(256, 1)
    before = positions[:, :1] - jnp.arange(512, 0, -1, dtype=jnp.int32)[None]
    places = jnp.concatenate([before, positions], axis=1).reshape(768, 1)
    steps = jnp.arange(128).astype(F32)
    angles = places.astype(F32) * (10000.0 ** (-2.0 * steps / 256))
    cos, sin = (jnp.cos(angles), jnp.sin(angles))
    m5, m2 = [jnp.asarray((np.arange(n) % k).astype(np.int32)) for n, k in ((640, 5), (256, 2))]

    gain_row = jnp.concatenate([norm_input, norm_post_attn, norm_pre_ff, norm_post_ff, norm_query, norm_key])
    gain_row = jnp.pad(gain_row, (0, 104)).reshape(1, 1, 128)
    flat = jnp.concatenate(
        [halves(w_query), halves(w_key), halves(w_value), jnp.broadcast_to(gain_row, (2, 1, 128))], axis=1
    )
    flat_ff = jnp.concatenate([halves(w_out), halves(w_gate), halves(w_up)], axis=1)
    near = lax.all_to_all(to_all(flat_ff, 2, 8), NEAR_Z, 0, 0)
    flat = jnp.concatenate([halves(w_down), flat], axis=1)
    near, flat, cos, sin, place = lax.optimization_barrier((near, flat, cos, sin, place))
    block = jnp.concatenate([block_of(near, 0, 3, 8), block_of(near, 24, 8, 5), block_of(near, 64, 8, 5)])
    f_own = lax.all_gather(block, "z")

    near = lax.all_to_all(to_all(flat, 8, 8), AXES, 0, 0)
    q_own, table = (block_of(near, 48, 6, 5), near[:, 78])
    q_own, x1, x2 = lax.optimization_barrier((q_own, x1, x2))
    q_oth = lax.ppermute(q_own, "core", SWAP)
    d_own = near[:, :48]
    d_oth = lax.ppermute(d_own, "core", SWAP)
    normed, q_raw, k_raw, q, kv, gains, attended, log_total = call(
        attend_kernel,
        [((768, 640), BF), ((4, 256, 256), F32), ((768, 256), F32), ((4, 256, 256), BF), ((768, 512), BF), ((8, 640), F32),
         ((4, 256, 256), BF), ((4, 256, 128), F32)],
        (core, x, x1, x2, q_own, q_oth, table, cos, sin, place, m5.reshape(1, 640), m2.reshape(1, 256)),
        name="attend",
    )
    f_own, attended = lax.optimization_barrier((f_own, attended))
    f_oth = lax.ppermute(f_own, "core", SWAP)
    mixed, d_hidden, d_att, d_gains, gff_own, gff_oth, gx_own, gx_oth = call(
        feed_kernel,
        [((256, 640), BF), ((256, 640), F32), ((4, 256, 256), BF), ((8, 640), F32)]
        + [((4, 2560, 128), BF)] * 2 + [((4, 32, 80, 128), BF)] * 2,
        (core, x, g, attended, gains, f_own, f_oth, d_own, d_oth),
        name="feed",
    )

    def both(mine, theirs):
        return (mine.astype(F32) + lax.ppermute(theirs.astype(BF), "core", SWAP).astype(F32)).astype(BF)

    gff, gx = (both(gff_own, gff_oth), both(gx_own, gx_oth)[:, :, :72])

    d_att, gff, gx = lax.optimization_barrier((d_att, gff, gx))
    d_q, dkv = call(
        attend_back_kernel,
        [((4, 256, 256), F32), ((768, 512), F32)],
        (q, kv, place, log_total, d_att),
        name="attend_back",
    )
    dx0, dx1, dx2, gq_own, gq_oth = call(
        project_back_kernel,
        [((256, 640), F32), ((256, 640), BF), ((256, 640), BF)] + [((4, 1120, 128), BF)] * 2,
        (core, x, x1, x2, normed, q_raw, k_raw, q_own, q_oth, cos, sin, gains, d_gains, m5.reshape(640, 1),
         m2.reshape(256, 1), d_q, dkv, d_hidden),
        name="project_back",
    )
    gq_got = lax.ppermute(gq_oth, "core", SWAP)
    gff_near = lax.psum_scatter(gff, "z")
    gx = lax.all_to_all(gx, Y, 0, 0)
    gq = (gq_own.astype(F32) + gq_got.astype(F32)).astype(BF)
    gq, gx, dx1, dx2, gff_near = lax.optimization_barrier((gq, gx, dx1, dx2, gff_near))

    gq_near = lax.psum_scatter(gq, "z")
    gx = lax.all_to_all(gx.astype(F32).sum(0).astype(BF), NEAR_Y, 0, 0)
    dx1, dx2 = (along(dx1, -1), along(dx2, -2))
    ff = pieces_of(gff_near, 16, 5)
    gx, dx1, dx2, ff, gq_near = lax.optimization_barrier((gx, dx1, dx2, ff, gq_near))
    rest = lax.all_to_all(jnp.concatenate([ff, pieces_of(gq_near, 7, 5)], axis=1), NEAR_Z, 0, 0)
    d_x = (dx0 + dx1.astype(F32) + dx2.astype(F32)).astype(BF)
    grads = call(
        finish_kernel,
        [((5, 1024), F32), ((5, 256), F32), ((5, 256), F32), ((8, 640), F32), ((5, 2048), F32), ((5, 2048), F32),
         ((16, 640), F32)] + [((1, n), F32) for n in GAINS],
        (rest, gx),
        scratch=(pltpu.VMEM((2, 120, 128), F32), pltpu.VMEM((2, 72, 128), F32)),
        name="finish",
    )
    grads = [g.reshape(-1) if g.shape[0] == 1 else g for g in grads]
    return (mixed.reshape(1, 256, 640), d_x.reshape(1, 256, 640), *grads)


def solution(mesh):
    fine = Mesh(mesh.devices.reshape([size for _, size in SIZES]), AXES)
    rows, lines, wide, flat = (P(DP, SEQ, None), P(DP, SEQ), P(AXES, None), P(AXES))
    return jax.shard_map(
        body,
        mesh=fine,
        in_specs=(rows, lines) + (wide,) * 7 + (flat,) * 6 + (rows,),
        out_specs=(rows, rows) + (wide,) * 7 + (flat,) * 6,
        check_vma=False,
    )
```
